128 devices in a mesh: ep: 16 (over x, z_hi, core), tp: 8 (over y, z_lo).
Axes of the slice: x: 4, y: 4, z: 4 (z_hi: 2, z_lo: 2; z = z_hi * 2 + z_lo), core: 2. Of those that a mesh axis runs over, the one named last changes fastest.
Arguments:
- tokens: bfloat16 [2048, 7168], P(('ep', 'tp')), may hold values from -6 to 6
- cotangent: bfloat16 [2048, 7168], P(('ep', 'tp')), may hold values from -6 to 6
- route_ids: int32 [2048, 2], P('ep'), may hold values from 0 to 63, all different within a row; in each aligned block of 128 rows (0 to 127, 128 to 255, ...) at most 6 rows name the same one
- route_probs: float32 [2048, 2], P('ep'), may hold values from 0.2 to 1
- dense_gate: bfloat16 [7168, 2432], P('ep', 'tp'), may hold values from -0.0625 to 0.0625
- dense_up: bfloat16 [7168, 2432], P('ep', 'tp'), may hold values from -0.0625 to 0.0625
- dense_down: bfloat16 [2432, 7168], P('tp', 'ep'), may hold values from -0.125 to 0.125
- expert_gate: bfloat16 [128, 192, 7168], P(('ep', 'tp')), may hold values from -0.0625 to 0.0625
- expert_up: bfloat16 [128, 192, 7168], P(('ep', 'tp')), may hold values from -0.0625 to 0.0625
- expert_down: bfloat16 [128, 192, 7168], P(('ep', 'tp')), may hold values from -0.3125 to 0.3125
Outputs:
- grad_tokens: bfloat16 [2048, 7168], P(('ep', 'tp'))
- grad_dense_gate: bfloat16 [7168, 2432], P('ep', 'tp')
- grad_dense_up: bfloat16 [7168, 2432], P('ep', 'tp')
- grad_dense_down: bfloat16 [2432, 7168], P('tp', 'ep')
- grad_expert_gate: bfloat16 [128, 192, 7168], P(('ep', 'tp'))
- grad_expert_up: bfloat16 [128, 192, 7168], P(('ep', 'tp'))
- grad_expert_down: bfloat16 [128, 192, 7168], P(('ep', 'tp'))
The draws below stay inside these ranges and needn't reach their ends.
Inputs may be any that keep to these rules, and one draw needn't show every extreme that they name: `route_ids`: each token names two different experts; within each aligned block of 128 tokens no expert is named more than 6 times, and in some block an expert is named exactly 6 times; every expert is named by some token.
All inputs are finite; a program needn't handle non-finite values.
Results may differ from the reference program's by a relative error of at most 0.024.
Values may be sent and summed in bfloat16 or wider, within the bound.
A program may use at most 128 MiB of HBM per device.

```python
import math
import jax
import jax.numpy as jnp
import numpy as np
from jax import lax

D = 7168
FF = 2432
EF = 384
HALF = 192
GROUP = 128
TOKENS = 2048
EXPERTS = 64
SLICES = 128
CAP = 6
N_EP = 16


def block_scale(rng, extent, cuts, smallest, largest):
    factor_of = 1.0
    for dim, parts in cuts:
        heights = jax.random.uniform(jax.random.fold_in(jax.random.fold_in(rng, 6), dim), (parts,), jnp.float32, smallest / len(cuts), largest / len(cuts))
        factor_of = factor_of * jnp.repeat(jnp.exp(heights), extent[dim] // parts).reshape((-1,) + (1,) * (len(extent) - 1 - dim))
    return factor_of


def assign_block(rng, own, number, rows, amount, top, bound, slope):
    ranking = jax.random.permutation(rng, amount)
    packed, ordinary = shares(amount, rows * top, bound, slope, True), shares(amount, rows * top, bound, slope, False)
    places = jnp.arange(amount)

    def named(sizes, rotation):
        used = int((sizes > 0).sum())
        fixed = max(1, used // 4)
        shifted = fixed + (places - fixed + rotation * (used - fixed)) % max(1, amount - fixed)
        return jnp.zeros((amount,), jnp.int32).at[ranking[jnp.where(places < fixed, places, shifted)]].set(jnp.asarray(sizes, jnp.int32))

    sizes = jnp.where(number % 4 == 0, named(packed, number // 4), named(ordinary, number - number // 4 - 1))
    mixed = jax.random.permutation(jax.random.fold_in(own, 3), amount)
    donor, taker = mixed[0:amount // 2 * 2:2], mixed[1:amount // 2 * 2:2]
    slack = jnp.minimum(sizes[donor] - 1, bound - sizes[taker]) // 2
    slack = jnp.where((donor == ranking[0]) | (taker == ranking[0]) | (sizes[taker] == 0), 0, jnp.maximum(slack, 0))
    shifted = jax.random.randint(jax.random.fold_in(own, 4), (amount // 2,), 0, 1 << 20) % (slack + 1)
    sizes = sizes.at[donor].add(-shifted).at[taker].add(shifted)
    members = jnp.searchsorted(jnp.cumsum(sizes), jnp.arange(rows * top), side="right").astype(jnp.int32)
    listing = members.reshape(top, rows).T
    listing = listing[jax.random.permutation(jax.random.fold_in(own, 1), rows)]
    rotation = jax.random.randint(jax.random.fold_in(own, 2), (rows, 1), 0, top)
    return jnp.take_along_axis(listing, (jnp.arange(top)[None, :] + rotation) % top, axis=1)


def shares(count, total, limit, lean, full):
    weights = [(1 << 20) // math.isqrt(rank ** lean) + 1 for rank in range(1, count + 1)]
    largest = limit if full else min(limit, max(-(-total // count), total * weights[0] // sum(weights)))
    least = 1 if total - largest >= count - 1 else 0
    counts, spare = [largest] + [least] * (count - 1), total - largest - least * (count - 1)
    while spare > 0:
        free = [i for i in range(1, count) if counts[i] < largest] or [i for i in range(1, count) if counts[i] < limit]
        whole, budget = sum([weights[i] for i in free]), spare
        for i in free:
            more = min(limit - counts[i], max(1, budget * weights[i] // whole), spare)
            counts[i] = counts[i] + more
            spare = spare - more
    return np.array(counts)


def gaussian(stream_key, shape, deviation, most, shards=(), held_as=jnp.bfloat16):
    result = deviation * jax.random.normal(stream_key, shape, jnp.float32)
    if shards:
        result = result * block_scale(stream_key, shape, shards, -0.22, 0.18)
    return jnp.clip(result, -most, most).astype(held_as)


def setup_inputs(seed: int = 0) -> dict:
    key_list = jax.random.split(jax.random.key(seed), 11)
    tokens = gaussian(key_list[0], (TOKENS, D), 1.0, 6.0, ((0, 128),))
    cotangent = gaussian(key_list[1], (TOKENS, D), 1.0, 6.0, ((0, 128),))
    route_ids_keys = jax.random.split(jax.random.fold_in(key_list[2], 1), TOKENS // GROUP)
    route_ids_turns = jax.random.permutation(jax.random.fold_in(key_list[2], 3), TOKENS // GROUP)
    route_ids = jax.vmap(lambda own, number: assign_block(jax.random.fold_in(key_list[2], 2), own, number, GROUP, EXPERTS, 2, CAP, 2))(route_ids_keys, route_ids_turns).reshape((TOKENS, 2))
    route_probs = jnp.clip(0.2 + 0.8 * jax.random.uniform(key_list[3], (TOKENS, 2), jnp.float32) ** block_scale(key_list[3], (TOKENS, 2), ((0, 16),), -0.2, 0.2), 0.2, 1.0)
    dense_gate = gaussian(key_list[4], (D, FF), D ** -0.5, 0.0625, ((0, 16), (1, 8)))
    dense_up = gaussian(key_list[5], (D, FF), D ** -0.5, 0.0625, ((0, 16), (1, 8)))
    dense_down = gaussian(key_list[6], (FF, D), FF ** -0.5, 0.125, ((0, 8), (1, 16)))
    expert_gate = gaussian(key_list[7], (SLICES, HALF, D), D ** -0.5, 0.0625, ((0, 128),))
    expert_up = gaussian(key_list[8], (SLICES, HALF, D), D ** -0.5, 0.0625, ((0, 128),))
    expert_down = gaussian(key_list[9], (SLICES, HALF, D), EF ** -0.5, 0.3125, ((0, 128),))
    return {"tokens": tokens, "cotangent": cotangent, "route_ids": route_ids, "route_probs": route_probs, "dense_gate": dense_gate, "dense_up": dense_up, "dense_down": dense_down, "expert_gate": expert_gate, "expert_up": expert_up, "expert_down": expert_down}


def product(left, right):
    return jnp.dot(left, right, preferred_element_type=jnp.float32)

def product_t(left, right):
    return lax.dot_general(left, right, (((1,), (1,)), ((), ())), preferred_element_type=jnp.float32)

def product_left(left, right):
    return lax.dot_general(left, right, (((0,), (0,)), ((), ())), preferred_element_type=jnp.float32)

def unit_grads(gate_pre, up_pre, d_hidden):
    sigmoid_gate = jax.nn.sigmoid(gate_pre)
    activated = gate_pre * sigmoid_gate
    hidden = (activated * up_pre).astype(jnp.bfloat16)
    d_gate = (d_hidden * up_pre * sigmoid_gate * (1.0 + gate_pre * (1.0 - sigmoid_gate))).astype(jnp.bfloat16)
    d_up = (d_hidden * activated).astype(jnp.bfloat16)
    return (hidden, d_gate, d_up)

def rounded_add(total, pieces):
    left, right = pieces
    term = lax.optimization_barrier(product_left(left, right).astype(jnp.bfloat16))
    return (total + term.astype(jnp.float32), None)

def reference(tokens, cotangent, route_ids, route_probs, dense_gate, dense_up, dense_down, expert_gate, expert_up, expert_down):
    pre_gate = product(tokens, dense_gate)
    pre_up = product(tokens, dense_up)
    dense_dh = product_t(cotangent, dense_down)
    dense_hidden, dense_dgate, dense_dup = unit_grads(pre_gate, pre_up, dense_dh)
    dense_dx = product_t(dense_dgate, dense_gate) + product_t(dense_dup, dense_up)
    token_blocks = tokens.reshape(N_EP, GROUP, D)
    cot_blocks = cotangent.reshape(N_EP, GROUP, D)
    gate_sum, _ = lax.scan(rounded_add, jnp.zeros((D, FF), jnp.float32), (token_blocks, dense_dgate.reshape(N_EP, GROUP, FF)))
    up_sum, _ = lax.scan(rounded_add, jnp.zeros((D, FF), jnp.float32), (token_blocks, dense_dup.reshape(N_EP, GROUP, FF)))
    down_sum, _ = lax.scan(rounded_add, jnp.zeros((FF, D), jnp.float32), (dense_hidden.reshape(N_EP, GROUP, FF), cot_blocks))
    scale_dense = 1.0 / math.sqrt(TOKENS)
    grad_dense_gate = (gate_sum * scale_dense).astype(jnp.bfloat16)
    grad_dense_up = (up_sum * scale_dense).astype(jnp.bfloat16)
    grad_dense_down = (down_sum * scale_dense).astype(jnp.bfloat16)
    scale_expert = math.sqrt(EXPERTS / (2.0 * TOKENS))
    slots = jnp.arange(CAP, dtype=jnp.int32)
    probs_blocks = route_probs.reshape(N_EP, 1, GROUP, 2)
    token_float = token_blocks.astype(jnp.float32)
    cot_float = cot_blocks.astype(jnp.float32)

    def expert_step(carry, expert_id):
        match = (route_ids == expert_id).astype(jnp.int32).reshape(N_EP, 2 * GROUP)
        rank = jnp.cumsum(match, axis=1, dtype=jnp.int32) - 1
        pick = ((rank[:, None, :] == slots[None, :, None]) & (match[:, None, :] == 1)).astype(jnp.float32)
        pick = pick.reshape(N_EP, CAP, GROUP, 2)
        select = lax.optimization_barrier(jnp.sum(pick, axis=3))
        slot_prob = lax.optimization_barrier(jnp.sum(pick * probs_blocks, axis=(2, 3)))
        rows_in = jnp.einsum('gcn,gnd->gcd', select, token_float).astype(jnp.bfloat16).reshape(N_EP * CAP, D)
        rows_cot = jnp.einsum('gcn,gnd->gcd', select, cot_float)
        rows_grad = (rows_cot * slot_prob[:, :, None]).astype(jnp.bfloat16).reshape(N_EP * CAP, D)
        gate_pair = lax.dynamic_slice_in_dim(expert_gate, 2 * expert_id, 2, 0)
        up_pair = lax.dynamic_slice_in_dim(expert_up, 2 * expert_id, 2, 0)
        down_pair = lax.dynamic_slice_in_dim(expert_down, 2 * expert_id, 2, 0)
        gate_whole = jnp.concatenate([gate_pair[0], gate_pair[1]], axis=0)
        up_whole = jnp.concatenate([up_pair[0], up_pair[1]], axis=0)
        down_whole = jnp.concatenate([down_pair[0], down_pair[1]], axis=0)
        expert_pre_gate = product_t(rows_in, gate_whole)
        expert_pre_up = product_t(rows_in, up_whole)
        expert_dh = product_t(rows_grad, down_whole)
        expert_hidden, expert_dgate, expert_dup = unit_grads(expert_pre_gate, expert_pre_up, expert_dh)
        grad_gate = (product_left(expert_dgate, rows_in) * scale_expert).astype(jnp.bfloat16)
        grad_up = (product_left(expert_dup, rows_in) * scale_expert).astype(jnp.bfloat16)
        grad_down = (product_left(expert_hidden, rows_grad) * scale_expert).astype(jnp.bfloat16)
        back_rows = product(expert_dgate, gate_whole) + product(expert_dup, up_whole)
        contrib = jnp.einsum('gcn,gcd->gnd', select, back_rows.reshape(N_EP, CAP, D))
        gate_halves = jnp.stack([grad_gate[:HALF], grad_gate[HALF:]])
        up_halves = jnp.stack([grad_up[:HALF], grad_up[HALF:]])
        down_halves = jnp.stack([grad_down[:HALF], grad_down[HALF:]])
        return (carry + contrib, (gate_halves, up_halves, down_halves))
    moe_sum, stacked = lax.scan(expert_step, jnp.zeros((N_EP, GROUP, D), jnp.float32), jnp.arange(EXPERTS, dtype=jnp.int32))
    grad_expert_gate = stacked[0].reshape(SLICES, HALF, D)
    grad_expert_up = stacked[1].reshape(SLICES, HALF, D)
    grad_expert_down = stacked[2].reshape(SLICES, HALF, D)
    grad_tokens = (cotangent.astype(jnp.float32) + dense_dx + moe_sum.reshape(TOKENS, D)).astype(jnp.bfloat16)
    return (grad_tokens, grad_dense_gate, grad_dense_up, grad_dense_down, grad_expert_gate, grad_expert_up, grad_expert_down)
```

```python
import functools
import math

import jax
import jax.numpy as jnp
from jax import lax
from jax.experimental import pallas as pl
from jax.experimental.pallas import tpu as pltpu
from jax.sharding import PartitionSpec as P

MESH = pl.DeviceIdType.MESH
F32 = jnp.float32
BF16 = jnp.bfloat16

NE, NT = 16, 8
GROUP, CAP = 128, 6
SLOTS = NE * CAP
HALF_SLOTS = SLOTS // 2
COVER = 512
FFB = 304
HID = 192


def dot_nt(a, b):
    return lax.dot_general(a, b, (((1,), (1,)), ((), ())), preferred_element_type=F32)


def dot_nn(a, b):
    return lax.dot_general(a, b, (((1,), (0,)), ((), ())), preferred_element_type=F32)


def dot_tn(a, b):
    return lax.dot_general(a, b, (((0,), (0,)), ((), ())), preferred_element_type=F32)


def unit_grads(gate_pre, up_pre, d_hidden):
    sigmoid_gate = jax.nn.sigmoid(gate_pre)
    activated = gate_pre * sigmoid_gate
    hidden = (activated * up_pre).astype(BF16)
    d_gate = (d_hidden * up_pre * sigmoid_gate * (1.0 + gate_pre * (1.0 - sigmoid_gate))).astype(BF16)
    d_up = (d_hidden * activated).astype(BF16)
    return hidden, d_gate, d_up


def cover_at(i):
    return pl.multiple_of(896 * (i // 2) + 384 * (i % 2), 128)


def kernel(
    scale_dense,
    tok, cot, route, wt, eg, eu, ed,
    gtok, gdense, eact, erows,
    xy, rr, part, c0r, x1r, x2r, z2r, hb, sel, sprob, ms, mr, we, eacc, bs, rb, dx, y1r, y2r, e2r, fs, fb, gacc,
    wsem, a_s, a_r, r_s, r_r, b_s, b_r, c0_s, c0_rs, c1_s, c1_rs, c2_s, c2_rs, d_s, d_r, m_s, m_r, e_s, e_r, f_s, f_r, osem,
):
    ep, tp = lax.axis_index("ep"), lax.axis_index("tp")
    x, zh, c = ep // 4, (ep // 2) % 2, ep % 2
    y, zl = tp // 2, tp % 2
    xp, xm, xo = (x + 1) % 4, (x + 3) % 4, (x + 2) % 4
    yp, ym, yo = (y + 1) % 4, (y + 3) % 4, (y + 2) % 4
    to_xp, to_xm = (ep + 4) % 16, (ep + 12) % 16
    dev_xp, dev_xm = (to_xp, tp), (to_xm, tp)
    dev_zh = ((x * 2 + 1 - zh) * 2 + c, tp)
    dev_core = ((x * 2 + zh) * 2 + 1 - c, tp)
    dev_yp, dev_ym = (ep, yp * 2 + zl), (ep, ym * 2 + zl)
    dev_zl = (ep, y * 2 + 1 - zl)

    def rc(src, dst, s, r, dev):
        return pltpu.make_async_remote_copy(
            src_ref=src, dst_ref=dst, send_sem=s, recv_sem=r, device_id=dev, device_id_type=MESH
        )

    def got(ref, r):
        rc(ref, ref, r, r, dev_core).wait_recv()

    def sent(ref, s):
        rc(ref, ref, s, s, dev_core).wait_send()

    loads = [pltpu.make_async_copy(w, we.at[n], wsem.at[n]) for n, w in enumerate((eg, eu, ed))]
    for w in loads:
        w.start()

    barrier = pltpu.get_barrier_semaphore()

    @pl.loop(1, NE)
    def _(k):
        pl.semaphore_signal(barrier, inc=1, device_id=((ep + k) % NE, tp), device_id_type=MESH)

    for d in (dev_yp, dev_ym, dev_zl):
        pl.semaphore_signal(barrier, inc=1, device_id=d, device_id_type=MESH)
    pl.semaphore_wait(barrier, NE - 1 + 3)

    srcs = (tok, cot)
    for a in range(2):

        @pl.loop(1, NE)
        def _(k):
            j = (ep + k) % NE
            rc(srcs[a].at[:, pl.ds(cover_at(j), COVER)], xy.at[a, ep, y, zl], a_s.at[a, k], a_r.at[a, k], (j, tp)).start()
            if a == 0:
                rc(route, rr.at[ep], r_s.at[k], r_r.at[k], (j, tp)).start()

        xy[a, ep, y, zl] = srcs[a][:, pl.ds(cover_at(ep), COVER)]
    rr[ep] = route[...]

    def blk(a, yy, zz):
        return xy.at[a, :, yy, zz]

    def lo(a, yy, zz):
        return xy.at[a, 0:8, yy, zz]

    def hi(a, yy, zz):
        return xy.at[a, 8:16, yy, zz]

    def send_b(a, n, ref, dev):
        rc(ref, ref, b_s.at[a, n], b_r.at[a, n], dev).start()

    for a in range(2):

        @pl.loop(1, NE)
        def _(k):
            i = (ep + NE - k) % NE
            got(xy.at[a, i, y, zl], a_r.at[a, k])

        send_b(a, 0, blk(a, y, zl), dev_zl)
        send_b(a, 1, blk(a, y, zl), dev_yp)
        send_b(a, 2, blk(a, y, zl), dev_ym)

    @pl.loop(1, NE)
    def _(k):
        got(rr.at[(ep + NE - k) % NE], r_r.at[k])

    base = ((tp // 2) * (2 * NE * HALF_SLOTS // 2)).astype(F32)
    for h in range(2):
        sprob[h] = jnp.zeros((NE * HALF_SLOTS, 128), F32)

        @pl.loop(0, 8)
        def _(gl):
            row = rr[h * 8 + gl]
            ids = lax.broadcasted_iota(jnp.int32, (NE * HALF_SLOTS, 128), 0).astype(F32)
            first = ids == (row[0:1] - base)
            second = ids == (row[1:2] - base)
            sel[h, :, pl.ds(pl.multiple_of(gl * 128, 128), 128)] = jnp.where(first | second, 1.0, 0.0).astype(BF16)
            sprob[h] += jnp.where(first, row[2:3], 0.0) + jnp.where(second, row[3:4], 0.0)

        sprob[h] = jnp.broadcast_to(jnp.sum(sprob[h], axis=1, keepdims=True), (NE * HALF_SLOTS, 128))

    def finish_b(a):
        got(blk(a, y, 1 - zl), b_r.at[a, 0])
        send_b(a, 3, blk(a, y, 1 - zl), dev_yp)
        send_b(a, 4, blk(a, y, 1 - zl), dev_ym)
        got(blk(a, ym, zl), b_r.at[a, 1])
        send_b(a, 5, lo(a, ym, zl), dev_yp)
        got(blk(a, yp, zl), b_r.at[a, 2])
        send_b(a, 6, hi(a, yp, zl), dev_ym)
        got(blk(a, ym, 1 - zl), b_r.at[a, 3])
        send_b(a, 7, lo(a, ym, 1 - zl), dev_yp)
        got(blk(a, yp, 1 - zl), b_r.at[a, 4])
        send_b(a, 8, hi(a, yp, 1 - zl), dev_ym)

    def end_b(a):
        got(lo(a, yo, zl), b_r.at[a, 5])
        got(hi(a, yo, zl), b_r.at[a, 6])
        got(lo(a, yo, 1 - zl), b_r.at[a, 7])
        got(hi(a, yo, 1 - zl), b_r.at[a, 8])

    spans = ((0, 2), (2, 3))

    def products(a):
        k0, k1 = spans[a]

        @pl.loop(0, 8)
        def _(p):
            rows = xy[a, pl.ds(2 * p, 2)].reshape(2 * GROUP, COVER)
            for k in range(k0, k1):
                res = dot_nt(wt[k], rows).astype(BF16)
                part[2 * p, k] = res[:, :GROUP]
                part[2 * p + 1, k] = res[:, GROUP:]
            rc(part.at[2 * p + 1 - c, k0:k1], c0r.at[p, k0:k1], c0_s.at[a, p], c0_rs.at[a, p], dev_core).start()

    def at1(buf, n, k0, k1):
        return buf.at[n, k0:k1]

    def at2(buf, n, m, k0, k1):
        return buf.at[n, m, k0:k1]

    def add(dst, srcs_):
        total = dst[...].astype(F32)
        for s in srcs_:
            total = total + s[...].astype(F32)
        dst[...] = total.astype(BF16)

    def sum_core(a):
        k0, k1 = spans[a]

        @pl.loop(0, 8)
        def _(p):
            got(c0r.at[p, k0:k1], c0_rs.at[a, p])
            for k in range(k0, k1):
                add(c0r.at[p, k], [part.at[2 * p + c, k]])

    def c1_sends(a):
        k0, k1 = spans[a]
        q = lambda xx, zz: c0r.at[xx * 2 + zz, k0:k1]
        return [
            rc(q(xo, 0), at1(x1r, 0, k0, k1), c1_s.at[a, 0], c1_rs.at[a, 0], dev_xp),
            rc(q(xo, 1), at1(x1r, 1, k0, k1), c1_s.at[a, 1], c1_rs.at[a, 1], dev_xm),
            rc(q(xp, 1), at2(x2r, 0, 1, k0, k1), c1_s.at[a, 2], c1_rs.at[a, 2], dev_xp),
            rc(q(xm, 0), at2(x2r, 1, 0, k0, k1), c1_s.at[a, 3], c1_rs.at[a, 3], dev_xm),
            rc(q(xp, 0), at2(x2r, 0, 0, k0, k1), c1_s.at[a, 4], c1_rs.at[a, 4], dev_xp),
            rc(q(xm, 1), at2(x2r, 1, 1, k0, k1), c1_s.at[a, 5], c1_rs.at[a, 5], dev_xm),
        ]

    def c1_first(a):
        for s in c1_sends(a)[:4]:
            s.start()

    def c1_second(a):
        k0, k1 = spans[a]
        sends = c1_sends(a)
        sends[0].wait_recv()
        for k in range(k0, k1):
            add(c0r.at[xp * 2, k], [x1r.at[0, k]])
        sends[4].start()
        sends[1].wait_recv()
        for k in range(k0, k1):
            add(c0r.at[xm * 2 + 1, k], [x1r.at[1, k]])
        sends[5].start()

    def c2_send(a):
        k0, k1 = spans[a]
        return rc(c0r.at[x * 2 + 1 - zh, k0:k1], z2r.at[k0:k1], c2_s.at[a], c2_rs.at[a], dev_zh)

    def c1_third(a):
        k0, k1 = spans[a]
        sends = c1_sends(a)
        for n in (2, 3, 4, 5):
            sends[n].wait_recv()
        for zz in (1 - zh, zh):
            for k in range(k0, k1):
                add(c0r.at[x * 2 + zz, k], [x2r.at[0, zz, k], x2r.at[1, zz, k]])
            if zz is not zh:
                c2_send(a).start()

    def routed(a):
        @pl.loop(0, 4)
        def _(n):
            jj = (x + n) % 4
            for h in range(2):
                rows = xy[a, 8 * h : 8 * h + 8].reshape(8 * GROUP, COVER)
                at = pl.multiple_of(jj * 4 * HALF_SLOTS, 64)
                res = dot_nn(sel[h, pl.ds(at, 4 * HALF_SLOTS)], rows)
                if a == 1:
                    res = res * sprob[h, pl.ds(at, 4 * HALF_SLOTS), 0:1]
                ms[a, pl.ds(jj * 4, 4), HALF_SLOTS * h : HALF_SLOTS * (h + 1)] = res.astype(BF16).reshape(4, HALF_SLOTS, COVER)

            @pl.loop(0, 4)
            def _(m):
                j = jj * 4 + m

                @pl.when(j != ep)
                def _():
                    rc(ms.at[a, j], mr.at[a, ep], m_s.at[a, j], m_r.at[a, ep], (j, tp)).start()

                @pl.when(j == ep)
                def _():
                    mr[a, j] = ms[a, j]

    def got_routed(a):
        @pl.loop(1, NE)
        def _(k):
            i = (ep + k) % NE
            got(mr.at[a, i], m_r.at[a, i])

    finish_b(0)
    end_b(0)
    products(0)
    finish_b(1)
    sum_core(0)
    c1_first(0)
    routed(0)
    end_b(1)
    products(1)
    sum_core(1)
    c1_first(1)
    c1_second(0)
    c1_second(1)
    c1_third(0)
    c1_third(1)
    for a in range(2):
        k0, k1 = spans[a]
        got(z2r.at[k0:k1], c2_rs.at[a])
    mine = [c0r[x * 2 + zh, k].astype(F32) + z2r[k].astype(F32) for k in range(3)]
    hidden, d_gate, d_up = unit_grads(*mine)
    hb[ep, 0] = d_gate
    hb[ep, 1] = d_up
    hb[ep, 2] = hidden

    def h_at(xx, zz):
        return hb.at[(xx * 2 + zz) * 2 + c]

    def send_d(n, ref, dev):
        rc(ref, ref, d_s.at[n], d_r.at[n], dev).start()

    def to_core(n, ref):
        rc(ref, ref, d_s.at[8 + n], d_r.at[8 + n], dev_core).start()

    own = h_at(x, zh)
    send_d(0, own, dev_zh)
    send_d(1, own, dev_xp)
    send_d(2, own, dev_xm)
    to_core(0, own)
    routed(1)
    got(h_at(x, 1 - zh), d_r.at[0])
    send_d(3, h_at(x, 1 - zh), dev_xp)
    send_d(4, h_at(x, 1 - zh), dev_xm)
    to_core(1, h_at(x, 1 - zh))
    got(h_at(xm, zh), d_r.at[1])
    send_d(5, h_at(xm, zh), dev_xp)
    to_core(2, h_at(xm, zh))
    got(h_at(xp, zh), d_r.at[2])
    to_core(3, h_at(xp, zh))
    got(h_at(xm, 1 - zh), d_r.at[3])
    to_core(4, h_at(xm, 1 - zh))
    got(h_at(xp, 1 - zh), d_r.at[4])
    send_d(6, h_at(xp, 1 - zh), dev_xm)
    to_core(5, h_at(xp, 1 - zh))
    got(h_at(xo, zh), d_r.at[5])
    to_core(6, h_at(xo, zh))
    got(h_at(xo, 1 - zh), d_r.at[6])
    to_core(7, h_at(xo, 1 - zh))

    for a in range(2):
        got_routed(a)
    for w in loads:
        w.wait()
    for n, a in enumerate((0, 0, 1)):
        total = jnp.zeros((SLOTS, HID), F32)
        for p in range(8):
            total += dot_nt(mr[a, 2 * p], we[n, :, 896 * p : 896 * p + 512])
            total += dot_nt(mr[a, 2 * p + 1, :, 128:512], we[n, :, 896 * p + 512 : 896 * p + 896])
        eacc[n] = total
    hidden, d_gate, d_up = unit_grads(eacc[0], eacc[1], eacc[2])
    eact[0] = d_gate
    eact[1] = d_up
    eact[2] = hidden

    @pl.loop(0, 8)
    def _(n):
        p = (ep // 2 + n) % 8
        at = pl.multiple_of(896 * p, 128)
        g, u = eact[0], eact[1]
        bs[2 * p] = (dot_nn(g, we[0, :, pl.ds(at, 512)]) + dot_nn(u, we[1, :, pl.ds(at, 512)])).astype(BF16)
        at2_ = pl.multiple_of(896 * p + 512, 128)
        bs[2 * p + 1, :, 0:128] = jnp.zeros((SLOTS, 128), BF16)
        bs[2 * p + 1, :, 128:512] = (
            dot_nn(g, we[0, :, pl.ds(at2_, 384)]) + dot_nn(u, we[1, :, pl.ds(at2_, 384)])
        ).astype(BF16)

        for m in range(2):
            i = 2 * p + m

            @pl.when(i != ep)
            def _():
                rc(bs.at[i], rb.at[ep], m_s.at[2, i], m_r.at[2, ep], (i, tp)).start()

            @pl.when(i == ep)
            def _():
                rb[i] = bs[i]

    outs = []
    for a in range(2):
        for p in range(8):
            outs.append(
                pltpu.make_async_copy(mr.at[a, 2 * p], erows.at[a, :, 896 * p : 896 * p + 512], osem.at[a, 2 * p])
            )
            outs.append(
                pltpu.make_async_copy(
                    mr.at[a, 2 * p + 1, :, 128:512], erows.at[a, :, 896 * p + 512 : 896 * p + 896], osem.at[a, 2 * p + 1]
                )
            )
    for o in outs:
        o.start()

    order = ((x, zh), (x, 1 - zh), (xm, zh), (xp, zh), (xm, 1 - zh), (xp, 1 - zh), (xo, zh), (xo, 1 - zh))
    for n, (xx, zz) in enumerate(order):
        got(hb.at[(xx * 2 + zz) * 2 + 1 - c], d_r.at[8 + n])

    got_routed_back = lambda: [got(rb.at[(ep + k) % NE], m_r.at[2, (ep + k) % NE]) for k in range(1, NE)]
    got_routed_back()
    for h in range(2):
        back = rb[:, HALF_SLOTS * h : HALF_SLOTS * (h + 1)].reshape(NE * HALF_SLOTS, COVER)

        @pl.loop(0, 4)
        def _(n):
            g = 8 * h + 2 * n
            s = sel[h, :, pl.ds(pl.multiple_of(n * 256, 256), 256)]
            total = dot_tn(s, back)
            for k in range(2):
                both = jnp.concatenate([hb[g, k], hb[g + 1, k]], axis=1)
                total = total + dot_tn(both, wt[k])
            dx[pl.ds(g, 2)] = total.astype(BF16).reshape(2, 4, 2, 16, COVER)

    def e_sends():
        return [
            rc(dx.at[0:8, yo], y1r.at[0], e_s.at[0], e_r.at[0], dev_yp),
            rc(dx.at[8:16, yo], y1r.at[1], e_s.at[1], e_r.at[1], dev_ym),
            rc(dx.at[8:16, yp], y2r.at[0, 8:16], e_s.at[2], e_r.at[2], dev_yp),
            rc(dx.at[0:8, ym], y2r.at[1, 0:8], e_s.at[3], e_r.at[3], dev_ym),
            rc(dx.at[0:8, yp], y2r.at[0, 0:8], e_s.at[4], e_r.at[4], dev_yp),
            rc(dx.at[8:16, ym], y2r.at[1, 8:16], e_s.at[5], e_r.at[5], dev_ym),
            rc(dx.at[:, y, 1 - zl], e2r, e_s.at[6], e_r.at[6], dev_zl),
        ]

    es = e_sends()
    for s in es[:4]:
        s.start()

    for k in range(3):
        gacc[...] = jnp.zeros((FFB, COVER), F32)

        @pl.loop(0, 4)
        def _(n):
            left = jnp.concatenate([hb[4 * n + m, k] for m in range(4)], axis=1)
            rows = xy[0 if k < 2 else 1, pl.ds(4 * n, 4)].reshape(4 * GROUP, COVER)
            gacc[...] += dot_nn(left, rows)

        gdense[k] = (gacc[...] * scale_dense).astype(BF16)

    es[0].wait_recv()
    add(dx.at[0:8, yp], [y1r.at[0]])
    es[4].start()
    es[1].wait_recv()
    add(dx.at[8:16, ym], [y1r.at[1]])
    es[5].start()
    for n in (2, 3, 4, 5):
        es[n].wait_recv()
    add(dx.at[:, y, 1 - zl], [y2r.at[0, :, 1 - zl], y2r.at[1, :, 1 - zl]])
    es[6].start()
    add(dx.at[:, y, zl], [y2r.at[0, :, zl], y2r.at[1, :, zl]])
    es[6].wait_recv()
    fs[...] = (dx[:, y, zl].astype(F32) + e2r[...].astype(F32)).astype(BF16)

    @pl.loop(1, NE)
    def _(k):
        j = (ep + k) % NE
        rc(fs.at[j], fb.at[ep], f_s.at[k], f_r.at[k], (j, tp)).start()

    fb[ep] = fs[ep]

    @pl.loop(1, NE)
    def _(k):
        got(fb.at[(ep + NE - k) % NE], f_r.at[k])

    for p in range(8):
        even, odd = fb[2 * p].astype(F32), fb[2 * p + 1].astype(F32)
        at = 896 * p
        gtok[:, at : at + 384] = (cot[:, at : at + 384].astype(F32) + even[:, 0:384]).astype(BF16)
        gtok[:, at + 384 : at + 512] = (
            cot[:, at + 384 : at + 512].astype(F32) + even[:, 384:512] + odd[:, 0:128]
        ).astype(BF16)
        gtok[:, at + 512 : at + 896] = (cot[:, at + 512 : at + 896].astype(F32) + odd[:, 128:512]).astype(BF16)

    for o in outs:
        o.wait()

    @pl.loop(1, NE)
    def _(k):
        j = (ep + k) % NE
        for a in range(2):
            sent(xy.at[a, ep, y, zl], a_s.at[a, k])
            sent(ms.at[a, j], m_s.at[a, j])
        sent(bs.at[j], m_s.at[2, j])
        sent(route, r_s.at[k])
        sent(fs.at[j], f_s.at[k])

    for a in range(2):
        for n in range(5):
            sent(blk(a, y, zl), b_s.at[a, n])
        for n in range(5, 9):
            sent(lo(a, y, zl), b_s.at[a, n])
        k0, k1 = spans[a]

        @pl.loop(0, 8)
        def _(p):
            sent(c0r.at[p, k0:k1], c0_s.at[a, p])

        for s in c1_sends(a):
            s.wait_send()
        c2_send(a).wait_send()

    @pl.loop(0, 7)
    def _(n):
        sent(own, d_s.at[n])

    @pl.loop(8, 16)
    def _(n):
        sent(own, d_s.at[n])

    for s in es:
        s.wait_send()


def exchange(tokens, cotangent, route, wt, eg, eu, ed, scale_dense):
    vm = lambda shape, dt=BF16: pltpu.VMEM(shape, dt)
    dma = lambda *shape: pltpu.SemaphoreType.DMA(shape)
    width = tokens.shape[1]
    vspec = pl.BlockSpec(memory_space=pltpu.VMEM)
    hspec = pl.BlockSpec(memory_space=pl.ANY)
    return pl.pallas_call(
        functools.partial(kernel, scale_dense),
        name="exchange",
        out_shape=(
            jax.ShapeDtypeStruct(tokens.shape, BF16),
            jax.ShapeDtypeStruct((3, FFB, COVER), BF16),
            jax.ShapeDtypeStruct((3, SLOTS, HID), BF16),
            jax.ShapeDtypeStruct((2, SLOTS, width), BF16),
        ),
        in_specs=[vspec] * 4 + [hspec] * 3,
        out_specs=(vspec, vspec, vspec, hspec),
        scratch_shapes=[
            vm((2, NE, 4, 2, 16, COVER)),
            vm((NE, 8, 128), F32),
            vm((NE, 3, FFB, GROUP)),
            vm((8, 3, FFB, GROUP)),
            vm((2, 3, FFB, GROUP)),
            vm((2, 2, 3, FFB, GROUP)),
            vm((3, FFB, GROUP)),
            vm((NE, 3, FFB, GROUP)),
            vm((2, NE * HALF_SLOTS, 8 * GROUP)),
            vm((2, NE * HALF_SLOTS, 128), F32),
            vm((2, NE, SLOTS, COVER)),
            vm((2, NE, SLOTS, COVER)),
            vm((3, HID, width)),
            vm((3, SLOTS, HID), F32),
            vm((NE, SLOTS, COVER)),
            vm((NE, SLOTS, COVER)),
            vm((NE, 4, 2, 16, COVER)),
            vm((2, 8, 2, 16, COVER)),
            vm((2, NE, 2, 16, COVER)),
            vm((NE, 16, COVER)),
            vm((NE, 16, COVER)),
            vm((NE, 16, COVER)),
            vm((FFB, COVER), F32),
            dma(3),
            dma(2, NE), dma(2, NE),
            dma(NE), dma(NE),
            dma(2, 9), dma(2, 9),
            dma(2, 8), dma(2, 8),
            dma(2, 6), dma(2, 6),
            dma(2), dma(2),
            dma(16), dma(16),
            dma(3, NE), dma(3, NE),
            dma(7), dma(7),
            dma(NE), dma(NE),
            dma(2, NE),
        ],
        compiler_params=pltpu.CompilerParams(
            collective_id=0, has_side_effects=True, vmem_limit_bytes=60 * 1024 * 1024
        ),
    )(tokens, cotangent, route, wt, eg, eu, ed)


def product_left(left, right):
    return lax.dot_general(left, right, (((0,), (0,)), ((), ())), preferred_element_type=F32)


def per_device(
    tokens, cotangent, route_ids, route_probs, dense_gate, dense_up, dense_down, expert_gate, expert_up, expert_down
):
    ep = lax.axis_index("ep")
    core = ep % 2
    total_tokens = NE * GROUP
    scale_dense = 1.0 / math.sqrt(total_tokens)
    scale_expert = math.sqrt(NE * NT // 2 / (2.0 * total_tokens))

    flat = route_ids.reshape(-1)
    place = jnp.arange(flat.shape[0])
    rank = jnp.sum((flat[:, None] == flat[None, :]) & (place[None, :] < place[:, None]), axis=1, dtype=jnp.int32)
    code = (flat % 4) * (NE * HALF_SLOTS) + (flat // 4) * HALF_SLOTS + (ep % 8) * CAP + rank
    code = code.reshape(GROUP, 2).astype(F32).T
    route = jnp.concatenate([code, route_probs.T, jnp.zeros((4, GROUP), F32)], axis=0)

    stacked = jnp.stack([dense_gate.T, dense_up.T, dense_down])
    pad = COVER - stacked.shape[2]
    wt = jnp.where(
        core == 0, jnp.pad(stacked, ((0, 0), (0, 0), (0, pad))), jnp.pad(stacked, ((0, 0), (0, 0), (pad, 0)))
    )
    gtok, gdense, eact, erows = exchange(
        tokens, cotangent, route, wt, expert_gate[0], expert_up[0], expert_down[0], scale_dense
    )
    gdense = jnp.where(core == 0, gdense[:, :, : COVER - pad], gdense[:, :, pad:])
    grads = [
        (product_left(eact[n], erows[a]) * scale_expert).astype(BF16)[None] for n, a in enumerate((0, 0, 1))
    ]
    return (gtok, gdense[0].T, gdense[1].T, gdense[2], *grads)


def solution(mesh):
    return jax.shard_map(
        per_device,
        mesh=mesh,
        in_specs=(
            P(("ep", "tp"), None),
            P(("ep", "tp"), None),
            P("ep", None),
            P("ep", None),
            P("ep", "tp"),
            P("ep", "tp"),
            P("tp", "ep"),
            P(("ep", "tp"), None, None),
            P(("ep", "tp"), None, None),
            P(("ep", "tp"), None, None),
        ),
        out_specs=(
            P(("ep", "tp"), None),
            P("ep", "tp"),
            P("ep", "tp"),
            P("tp", "ep"),
            P(("ep", "tp"), None, None),
            P(("ep", "tp"), None, None),
            P(("ep", "tp"), None, None),
        ),
        check_vma=False,
    )
```

```python
import functools
import math

import jax
import jax.numpy as jnp
from jax import lax
from jax.experimental import pallas as pl
from jax.experimental.pallas import tpu as pltpu
from jax.sharding import PartitionSpec as P

MESH = pl.DeviceIdType.MESH
F32 = jnp.float32
BF16 = jnp.bfloat16

NE, NT = 16, 8
GROUP, CAP = 128, 6
SLOTS = NE * CAP
HALF_SLOTS = SLOTS // 2
COVER = 512
FFB = 304
HID = 192


def dot_nt(a, b):
    return lax.dot_general(a, b, (((1,), (1,)), ((), ())), preferred_element_type=F32)


def dot_nn(a, b):
    return lax.dot_general(a, b, (((1,), (0,)), ((), ())), preferred_element_type=F32)


def dot_tn(a, b):
    return lax.dot_general(a, b, (((0,), (0,)), ((), ())), preferred_element_type=F32)


def unit_grads(gate_pre, up_pre, d_hidden):
    sigmoid_gate = jax.nn.sigmoid(gate_pre)
    activated = gate_pre * sigmoid_gate
    hidden = (activated * up_pre).astype(BF16)
    d_gate = (d_hidden * up_pre * sigmoid_gate * (1.0 + gate_pre * (1.0 - sigmoid_gate))).astype(BF16)
    d_up = (d_hidden * activated).astype(BF16)
    return hidden, d_gate, d_up


def kernel(
    scale_dense,
    tok, cot, ids, probs, dgate, dup, ddown, eg, eu, ed,
    gtok, gdense, eact, erows,
    xy, route, rr, wt, part, c0r, x1r, x2r, z2r, hb, sel, sprob, ms, mr, we, eacc, bs, rb, dx, er, fs, fb, gacc,
    wsem, a_s, a_r, r_s, r_r, b_s, b_r, c0_s, c0_rs, c1_s, c1_rs, c2_s, c2_rs, d_s, d_r, m_s, m_r, e_s, e_r, f_s, f_r, k_s, k_r, osem,
):
    ep, tp = lax.axis_index("ep"), lax.axis_index("tp")
    x, zh, c = ep // 4, (ep // 2) % 2, ep % 2
    y, zl = tp // 2, tp % 2
    xo, xs, xr = (x + 2) % 4, (x + 1 + 2 * c) % 4, (x + 3 + 2 * c) % 4
    yo, ys, yr = (y + 2) % 4, (y + 1 + 2 * c) % 4, (y + 3 + 2 * c) % 4

    full, rest = slice(0, COVER), slice(128, COVER)

    def by_core(act):
        pl.when(c == 0)(lambda: act(full))
        pl.when(c == 1)(lambda: act(rest))

    def dev_x(xx):
        return ((xx * 2 + zh) * 2 + c, tp)

    def dev_y(yy):
        return (ep, yy * 2 + zl)

    dev_zh = ((x * 2 + 1 - zh) * 2 + c, tp)
    dev_core = ((x * 2 + zh) * 2 + 1 - c, tp)
    dev_zl = (ep, y * 2 + 1 - zl)

    def rc(src, dst, s, r, dev):
        return pltpu.make_async_remote_copy(
            src_ref=src, dst_ref=dst, send_sem=s, recv_sem=r, device_id=dev, device_id_type=MESH
        )

    def got(ref, r):
        rc(ref, ref, r, r, dev_core).wait_recv()

    def sent(ref, s):
        rc(ref, ref, s, s, dev_core).wait_send()

    def add(dst, srcs_):
        total = dst[...].astype(F32)
        for s in srcs_:
            total = total + s[...].astype(F32)
        dst[...] = total.astype(BF16)

    loads = [pltpu.make_async_copy(w, we.at[n], wsem.at[n]) for n, w in enumerate((eg, eu, ed))]
    for w in loads:
        w.start()

    @pl.when(c == 1)
    def _():
        rb[:, :, 0:128] = jnp.zeros((NE, SLOTS, 128), BF16)

    barrier = pltpu.get_barrier_semaphore()

    @pl.loop(1, NE)
    def _(k):
        pl.semaphore_signal(barrier, inc=1, device_id=((ep + k) % NE, tp), device_id_type=MESH)

    @pl.loop(1, NT)
    def _(k):
        pl.semaphore_signal(barrier, inc=1, device_id=(ep, (tp + k) % NT), device_id_type=MESH)


    pl.semaphore_wait(barrier, NE - 1 + NT - 1)

    srcs = (tok, cot)

    def a_copy(a, k):
        j = (ep + k) % NE
        at = pl.multiple_of(896 * (j // 2) + 512 * (j % 2), 128)
        return lambda lanes: rc(
            srcs[a].at[:, pl.ds(at, lanes.stop - lanes.start)],
            xy.at[a, ep, y, zl, :, lanes], a_s.at[a, k], a_r.at[a, k], (j, tp),
        )

    def a_send(a):
        @pl.loop(1, NE)
        def _(k):
            pl.when((ep + k) % 2 == 0)(lambda: a_copy(a, k)(full).start())
            pl.when((ep + k) % 2 == 1)(lambda: a_copy(a, k)(rest).start())

        @pl.when(c == 0)
        def _():
            xy[a, ep, y, zl] = srcs[a][:, pl.ds(pl.multiple_of(896 * (ep // 2), 128), 512)]

        @pl.when(c == 1)
        def _():
            xy[a, ep, y, zl, :, 128:512] = srcs[a][:, pl.ds(pl.multiple_of(896 * (ep // 2) + 512, 128), 384)]

    a_send(0)

    before = lax.broadcasted_iota(jnp.int32, (GROUP, GROUP), 0) < lax.broadcasted_iota(jnp.int32, (GROUP, GROUP), 1)
    across = [jnp.broadcast_to(ids[k : k + 1, :].astype(F32), (GROUP, GROUP)) for k in range(2)]
    down = [jnp.transpose(m) for m in across]
    codes = []
    for k in range(2):
        rank = jnp.zeros((1, GROUP), F32)
        for m in down:
            rank = rank + jnp.sum(jnp.where(before & (m == across[k]), 1.0, 0.0), axis=0, keepdims=True)
        idk = ids[k : k + 1, :]
        group_at = (ep % 8) * CAP
        fixed = (idk & 3) * (NE * HALF_SLOTS) + (idk >> 2) * HALF_SLOTS + group_at
        codes.append(fixed.astype(F32) + rank)
    route[...] = jnp.concatenate([codes[0], codes[1], probs[...], jnp.zeros((4, GROUP), F32)], axis=0)

    @pl.loop(1, NE)
    def _(k):
        rc(route, rr.at[ep], r_s.at[k], r_r.at[k], ((ep + k) % NE, tp)).start()

    a_send(1)
    blank = jnp.zeros((FFB, COVER - 448), BF16)

    @pl.when(c == 0)
    def _():
        for k, w in enumerate((dgate, dup, ddown)):
            wt[k] = jnp.concatenate([w[...], blank], axis=1)

    @pl.when(c == 1)
    def _():
        for k, w in enumerate((dgate, dup, ddown)):
            wt[k] = jnp.concatenate([blank, w[...]], axis=1)

    rr[ep] = route[...]

    def got_a(a):
        @pl.loop(1, NE)
        def _(k):
            i = (ep + NE - k) % NE
            by_core(lambda lanes: got(xy.at[a, i, y, zl, :, lanes], a_r.at[a, k]))

    def send_b(a, h, n, yy, zz, dev):
        def act(lanes):
            ref = xy.at[a, 8 * h : 8 * h + 8, yy, zz, :, lanes]
            rc(ref, ref, b_s.at[2 * a + h, n], b_r.at[2 * a + h, n], dev).start()

        by_core(act)

    def got_b(a, h, n, yy, zz):
        by_core(lambda lanes: got(xy.at[a, 8 * h : 8 * h + 8, yy, zz, :, lanes], b_r.at[2 * a + h, n]))

    def sent_b(a, h, n):
        by_core(lambda lanes: sent(xy.at[a, 8 * h : 8 * h + 8, y, zl, :, lanes], b_s.at[2 * a + h, n]))

    def b_zero(a):
        for h in range(2):
            send_b(a, h, 0, y, zl, dev_zl)

    def b_first(a, h):
        send_b(a, h, 1, y, zl, dev_y(ys))
        send_b(a, h, 2, y, zl, dev_y(yr))

    def b_mid(a, h):
        got_b(a, h, 0, y, 1 - zl)
        send_b(a, h, 3, y, 1 - zl, dev_y(ys))
        send_b(a, h, 4, y, 1 - zl, dev_y(yr))

    def b_forward(a, h, second):
        if second:
            got_b(a, h, 3, yr, 1 - zl)
            send_b(a, h, 6, yr, 1 - zl, dev_y(ys))
        else:
            got_b(a, h, 1, yr, zl)
            send_b(a, h, 5, yr, zl, dev_y(ys))
            got_b(a, h, 2, ys, zl)

    def shared(a, h, at):
        return xy.at[a, 8 * h : 8 * h + 8, :, :, :, at : at + 128]

    def b_end(a, h):
        got_b(a, h, 5, yo, zl)
        got_b(a, h, 4, ys, 1 - zl)
        got_b(a, h, 6, yo, 1 - zl)

        @pl.when(c == 0)
        def _():
            rc(shared(a, h, 384), shared(a, h, 0), k_s.at[2 * a + h], k_r.at[2 * a + h], dev_core).start()

        @pl.when(c == 1)
        def _():
            got(shared(a, h, 0), k_r.at[2 * a + h])

    def slots():
        @pl.loop(1, NE)
        def _(k):
            got(rr.at[(ep + NE - k) % NE], r_r.at[k])

        base = ((tp // 2) * (NE * HALF_SLOTS)).astype(F32)
        for h in range(2):
            sprob[h] = jnp.zeros((NE * HALF_SLOTS, 128), F32)

            @pl.loop(0, 8)
            def _(gl):
                row = rr[h * 8 + gl]
                numbers = lax.broadcasted_iota(jnp.int32, (NE * HALF_SLOTS, 128), 0).astype(F32)
                first = numbers == (row[0:1] - base)
                second = numbers == (row[1:2] - base)
                sel[h, :, pl.ds(pl.multiple_of(gl * 128, 128), 128)] = jnp.where(first | second, 1.0, 0.0).astype(BF16)
                sprob[h] += jnp.where(first, row[2:3], 0.0) + jnp.where(second, row[3:4], 0.0)

            sprob[h] = jnp.broadcast_to(jnp.sum(sprob[h], axis=1, keepdims=True), (NE * HALF_SLOTS, 128))

    spans = ((0, 2), (2, 3))

    def products(a):
        k0, k1 = spans[a]

        @pl.loop(0, 8)
        def _(p):
            rows = xy[a, pl.ds(2 * p, 2)].reshape(2 * GROUP, COVER)
            for k in range(k0, k1):
                res = dot_nt(wt[k], rows).astype(BF16)
                part[2 * p, k] = res[:, :GROUP]
                part[2 * p + 1, k] = res[:, GROUP:]
            rc(
                part.at[2 * p + 1 - c, k0:k1], c0r.at[p // 2, p % 2, k0:k1], c0_s.at[a, p], c0_rs.at[a, p], dev_core
            ).start()

    def sum_core(a):
        k0, k1 = spans[a]

        @pl.loop(0, 8)
        def _(p):
            got(c0r.at[p // 2, p % 2, k0:k1], c0_rs.at[a, p])
            for k in range(k0, k1):
                add(c0r.at[p // 2, p % 2, k], [part.at[2 * p + c, k]])

    def c1_sends(a):
        k0, k1 = spans[a]
        q = lambda xx: c0r.at[xx, :, k0:k1]
        return [
            rc(q(xo), x1r.at[:, k0:k1], c1_s.at[a, 0], c1_rs.at[a, 0], dev_x(xs)),
            rc(q(xr), x2r.at[1, :, k0:k1], c1_s.at[a, 1], c1_rs.at[a, 1], dev_x(xr)),
            rc(q(xs), x2r.at[0, :, k0:k1], c1_s.at[a, 2], c1_rs.at[a, 2], dev_x(xs)),
        ]

    def c1_first(a):
        for s in c1_sends(a)[:2]:
            s.start()

    def c1_second(a):
        k0, k1 = spans[a]
        sends = c1_sends(a)
        sends[0].wait_recv()
        for zz in range(2):
            for k in range(k0, k1):
                add(c0r.at[xs, zz, k], [x1r.at[zz, k]])
        sends[2].start()

    def c2_send(a):
        k0, k1 = spans[a]
        return rc(c0r.at[x, 1 - zh, k0:k1], z2r.at[k0:k1], c2_s.at[a], c2_rs.at[a], dev_zh)

    def c1_third(a):
        k0, k1 = spans[a]
        sends = c1_sends(a)
        for n in (1, 2):
            sends[n].wait_recv()
        for n, zz in enumerate((1 - zh, zh)):
            for k in range(k0, k1):
                add(c0r.at[x, zz, k], [x2r.at[0, zz, k], x2r.at[1, zz, k]])
            if n == 0:
                c2_send(a).start()

    def rows_of(h):
        return slice(HALF_SLOTS * h, HALF_SLOTS * (h + 1))

    def m_copy(a, h, j, lanes):
        return rc(
            ms.at[a, j, rows_of(h), lanes], mr.at[a, ep, rows_of(h), lanes], m_s.at[2 * a + h, j], m_r.at[2 * a + h, ep], (j, tp)
        )

    def routed(a, h):
        @pl.loop(0, 4)
        def _(n):
            jj = (x + n) % 4
            rows = xy[a, 8 * h : 8 * h + 8].reshape(8 * GROUP, COVER)
            at = pl.multiple_of(jj * 4 * HALF_SLOTS, 64)
            res = dot_nn(sel[h, pl.ds(at, 4 * HALF_SLOTS)], rows)
            if a == 1:
                res = res * sprob[h, pl.ds(at, 4 * HALF_SLOTS), 0:1]
            ms[a, pl.ds(jj * 4, 4), rows_of(h)] = res.astype(BF16).reshape(4, HALF_SLOTS, COVER)

            @pl.loop(0, 4)
            def _(m):
                j = jj * 4 + m

                @pl.when((j != ep) & (c == 0))
                def _():
                    m_copy(a, h, j, full).start()

                @pl.when((j != ep) & (c == 1))
                def _():
                    m_copy(a, h, j, rest).start()

                @pl.when(j == ep)
                def _():
                    mr[a, j, rows_of(h)] = ms[a, j, rows_of(h)]

    def got_routed(a, h):
        @pl.loop(0, 8)
        def _(p):
            @pl.when(2 * p != ep)
            def _():
                got(mr.at[a, 2 * p, rows_of(h)], m_r.at[2 * a + h, 2 * p])

            @pl.when(2 * p + 1 != ep)
            def _():
                got(mr.at[a, 2 * p + 1, rows_of(h), rest], m_r.at[2 * a + h, 2 * p + 1])

    def expert_forward(h):
        for a in range(2):
            got_routed(a, h)
        if h == 0:
            for w in loads:
                w.wait()
        for n, a in enumerate((0, 0, 1)):
            total = jnp.zeros((HALF_SLOTS, HID), F32)
            for p in range(8):
                total += dot_nt(mr[a, 2 * p, rows_of(h)], we[n, :, 896 * p : 896 * p + 512])
                total += dot_nt(mr[a, 2 * p + 1, rows_of(h), rest], we[n, :, 896 * p + 512 : 896 * p + 896])
            eacc[n] = total
        hidden, d_gate, d_up = unit_grads(eacc[0], eacc[1], eacc[2])
        eact[0, rows_of(h)] = d_gate
        eact[1, rows_of(h)] = d_up
        eact[2, rows_of(h)] = hidden

    def back_copy(h, i, lanes):
        return rc(bs.at[i, rows_of(h), lanes], rb.at[ep, rows_of(h), lanes], m_s.at[4 + h, i], m_r.at[4 + h, ep], (i, tp))

    def expert_back(h):
        @pl.loop(0, 8)
        def _(n):
            p = (ep // 2 + n) % 8
            g, u = eact[0, rows_of(h)], eact[1, rows_of(h)]
            for m, lanes in enumerate((full, rest)):
                i = 2 * p + m
                wide = pl.ds(pl.multiple_of(896 * p + 512 * m, 128), 512 - 128 * m)
                bs[i, rows_of(h), lanes] = (dot_nn(g, we[0, :, wide]) + dot_nn(u, we[1, :, wide])).astype(BF16)

                @pl.when(i != ep)
                def _():
                    back_copy(h, i, lanes).start()

                @pl.when(i == ep)
                def _():
                    rb[i, rows_of(h), lanes] = bs[i, rows_of(h), lanes]

    def got_back(h):
        @pl.loop(1, NE)
        def _(k):
            j = (ep + k) % NE

            @pl.when(c == 0)
            def _():
                got(rb.at[j, rows_of(h)], m_r.at[4 + h, j])

            @pl.when(c == 1)
            def _():
                got(rb.at[j, rows_of(h), rest], m_r.at[4 + h, j])

    def h_at(xx, zz):
        return hb.at[(xx * 2 + zz) * 2 + c]

    def send_d(n, xx, zz, dev):
        rc(h_at(xx, zz), h_at(xx, zz), d_s.at[n], d_r.at[n], dev).start()

    def got_d(n, xx, zz):
        got(h_at(xx, zz), d_r.at[n])

    def to_core(n, xx, zz):
        send_d(7 + n, xx, zz, dev_core)

    def d_first():
        for a in range(2):
            k0, k1 = spans[a]
            got(z2r.at[k0:k1], c2_rs.at[a])
        mine = [c0r[x, zh, k].astype(F32) + z2r[k].astype(F32) for k in range(3)]
        hidden, d_gate, d_up = unit_grads(*mine)
        hb[ep, 0] = d_gate
        hb[ep, 1] = d_up
        hb[ep, 2] = hidden
        send_d(0, x, zh, dev_zh)
        send_d(1, x, zh, dev_x(xs))
        send_d(2, x, zh, dev_x(xr))
        to_core(0, x, zh)

    def d_mid():
        got_d(0, x, 1 - zh)
        send_d(3, x, 1 - zh, dev_x(xs))
        send_d(4, x, 1 - zh, dev_x(xr))
        to_core(1, x, 1 - zh)

    def d_forward():
        got_d(1, xr, zh)
        send_d(5, xr, zh, dev_x(xs))
        to_core(2, xr, zh)
        got_d(3, xr, 1 - zh)
        send_d(6, xr, 1 - zh, dev_x(xs))
        to_core(3, xr, 1 - zh)

    def d_end():
        got_d(2, xs, zh)
        to_core(4, xs, zh)
        got_d(4, xs, 1 - zh)
        to_core(5, xs, 1 - zh)
        got_d(5, xo, zh)
        to_core(6, xo, zh)
        got_d(6, xo, 1 - zh)
        to_core(7, xo, 1 - zh)
        sx = (x + 1 + 2 * c) % 4
        sr = (x + 3 + 2 * c) % 4
        for n, (xx, zz) in enumerate(
            ((x, zh), (x, 1 - zh), (sx, zh), (sx, 1 - zh), (sr, zh), (sr, 1 - zh), (xo, zh), (xo, 1 - zh))
        ):
            got(hb.at[(xx * 2 + zz) * 2 + 1 - c], d_r.at[7 + n])

    def input_grads(h):
        @pl.loop(0, 4)
        def _(n):
            g = 8 * h + 2 * n
            back = rb[:, rows_of(h)].reshape(NE * HALF_SLOTS, COVER)
            total = dot_tn(sel[h, :, pl.ds(pl.multiple_of(n * 256, 256), 256)], back)
            for k in range(2):
                both = jnp.concatenate([hb[g, k], hb[g + 1, k]], axis=1)
                total = total + dot_tn(both, wt[k])
            dx[pl.ds(g, 2)] = total.astype(BF16).reshape(2, 4, 2, 16, COVER)

    def e_copy(h, t):
        return rc(dx.at[8 * h : 8 * h + 8, t // 2, t % 2], er.at[h, tp], e_s.at[h, t], e_r.at[h, tp], (ep, t))

    def e_start(h):
        @pl.loop(1, NT)
        def _(k):
            e_copy(h, (tp + k) % NT).start()

    def f_copy(j):
        return rc(fs.at[j], fb.at[ep], f_s.at[j], f_r.at[ep], (j, tp))

    def e_last(h):
        @pl.loop(1, NT)
        def _(k):
            t = (tp + k) % NT
            got(er.at[h, t], e_r.at[h, t])

        half = slice(8 * h, 8 * h + 8)
        er[h, tp] = dx[half, y, zl]
        total = er[h, 0].astype(F32)
        for t in range(1, NT):
            total = total + er[h, t].astype(F32)
        fs[half] = total.astype(BF16)

        @pl.loop(0, 8)
        def _(n):
            j = 8 * h + (ep + n) % 8

            @pl.when(j != ep)
            def _():
                f_copy(j).start()

            @pl.when(j == ep)
            def _():
                fb[j] = fs[j]

    def weight_grads(k):
        gacc[...] = jnp.zeros((FFB, COVER), F32)

        @pl.loop(0, 4)
        def _(n):
            left = jnp.concatenate([hb[4 * n + m, k] for m in range(4)], axis=1)
            rows = xy[0 if k < 2 else 1, pl.ds(4 * n, 4)].reshape(4 * GROUP, COVER)
            gacc[...] += dot_nn(left, rows)

        gdense[k] = (gacc[...] * scale_dense).astype(BF16)

    got_a(0)
    b_zero(0)
    b_first(0, 0)
    b_first(0, 1)
    got_a(1)
    b_zero(1)
    slots()
    b_mid(0, 0)
    b_forward(0, 0, False)
    b_forward(0, 0, True)
    b_mid(0, 1)
    b_first(1, 0)
    b_forward(0, 1, False)
    b_end(0, 0)
    routed(0, 0)
    b_forward(0, 1, True)
    b_mid(1, 0)
    b_first(1, 1)
    b_end(0, 1)
    products(0)
    b_forward(1, 0, False)
    sum_core(0)
    c1_first(0)
    b_forward(1, 0, True)
    routed(0, 1)
    b_mid(1, 1)
    b_forward(1, 1, False)
    c1_second(0)
    b_end(1, 0)
    routed(1, 0)
    b_forward(1, 1, True)
    c1_third(0)
    b_end(1, 1)
    products(1)
    sum_core(1)
    c1_first(1)
    routed(1, 1)
    c1_second(1)
    expert_forward(0)
    c1_third(1)
    expert_back(0)
    d_first()
    expert_forward(1)
    d_mid()
    expert_back(1)

    outs = []
    for a in range(2):
        for p in range(8):
            for m, lanes in enumerate((full, rest)):
                at = 896 * p + 512 * m
                outs.append(
                    pltpu.make_async_copy(
                        mr.at[a, 2 * p + m, :, lanes], erows.at[a, :, at : at + 512 - 128 * m], osem.at[a, 2 * p + m]
                    )
                )
    for o in outs:
        o.start()

    d_forward()
    d_end()
    got_back(0)
    input_grads(0)
    e_start(0)
    weight_grads(0)
    got_back(1)
    input_grads(1)
    e_start(1)
    weight_grads(1)
    e_last(0)
    weight_grads(2)
    e_last(1)

    @pl.loop(1, NE)
    def _(k):
        i = (ep + k) % NE
        got(fb.at[i], f_r.at[i])

    for p in range(8):
        even, odd = fb[2 * p].astype(F32), fb[2 * p + 1].astype(F32)
        at = 896 * p
        gtok[:, at : at + 384] = (cot[:, at : at + 384].astype(F32) + even[:, 0:384]).astype(BF16)
        gtok[:, at + 384 : at + 512] = (
            cot[:, at + 384 : at + 512].astype(F32) + even[:, 384:512] + odd[:, 0:128]
        ).astype(BF16)
        gtok[:, at + 512 : at + 896] = (cot[:, at + 512 : at + 896].astype(F32) + odd[:, 128:512]).astype(BF16)

    for o in outs:
        o.wait()

    @pl.loop(1, NE)
    def _(k):
        j = (ep + k) % NE
        for a in range(2):
            pl.when(j % 2 == 0)(lambda: a_copy(a, k)(full).wait_send())
            pl.when(j % 2 == 1)(lambda: a_copy(a, k)(rest).wait_send())
        sent(route, r_s.at[k])
        f_copy(j).wait_send()
        for h in range(2):
            for a in range(2):

                @pl.when(c == 0)
                def _():
                    m_copy(a, h, j, full).wait_send()

                @pl.when(c == 1)
                def _():
                    m_copy(a, h, j, rest).wait_send()

            @pl.when(j % 2 == 0)
            def _():
                back_copy(h, j, full).wait_send()

            @pl.when(j % 2 == 1)
            def _():
                back_copy(h, j, rest).wait_send()

    for a in range(2):
        for h in range(2):
            for n in range(7):
                sent_b(a, h, n)

            @pl.when(c == 0)
            def _():
                sent(shared(a, h, 384), k_s.at[2 * a + h])

        k0, k1 = spans[a]

        @pl.loop(0, 8)
        def _(p):
            sent(c0r.at[p // 2, p % 2, k0:k1], c0_s.at[a, p])

        for s in c1_sends(a):
            s.wait_send()
        c2_send(a).wait_send()

    @pl.loop(0, 15)
    def _(n):
        sent(h_at(x, zh), d_s.at[n])

    @pl.loop(1, NT)
    def _(k):
        for h in range(2):
            e_copy(h, (tp + k) % NT).wait_send()


def exchange(tokens, cotangent, ids, probs, dgate, dup, ddown, eg, eu, ed, scale_dense):
    vm = lambda shape, dt=BF16: pltpu.VMEM(shape, dt)
    dma = lambda *shape: pltpu.SemaphoreType.DMA(shape)
    width = tokens.shape[1]
    vspec = pl.BlockSpec(memory_space=pltpu.VMEM)
    hspec = pl.BlockSpec(memory_space=pl.ANY)
    return pl.pallas_call(
        functools.partial(kernel, scale_dense),
        name="exchange",
        out_shape=(
            jax.ShapeDtypeStruct(tokens.shape, BF16),
            jax.ShapeDtypeStruct((3, FFB, COVER), BF16),
            jax.ShapeDtypeStruct((3, SLOTS, HID), BF16),
            jax.ShapeDtypeStruct((2, SLOTS, width), BF16),
        ),
        in_specs=[vspec] * 7 + [hspec] * 3,
        out_specs=(vspec, vspec, vspec, hspec),
        scratch_shapes=[
            vm((2, NE, 4, 2, 16, COVER)),
            vm((8, GROUP), F32),
            vm((NE, 8, GROUP), F32),
            vm((3, FFB, COVER)),
            vm((NE, 3, FFB, GROUP)),
            vm((4, 2, 3, FFB, GROUP)),
            vm((2, 3, FFB, GROUP)),
            vm((2, 2, 3, FFB, GROUP)),
            vm((3, FFB, GROUP)),
            vm((NE, 3, FFB, GROUP)),
            vm((2, NE * HALF_SLOTS, 8 * GROUP)),
            vm((2, NE * HALF_SLOTS, 128), F32),
            vm((2, NE, SLOTS, COVER)),
            vm((2, NE, SLOTS, COVER)),
            vm((3, HID, width)),
            vm((3, HALF_SLOTS, HID), F32),
            vm((NE, SLOTS, COVER)),
            vm((NE, SLOTS, COVER)),
            vm((NE, 4, 2, 16, COVER)),
            vm((2, NT, 8, 16, COVER)),
            vm((NE, 16, COVER)),
            vm((NE, 16, COVER)),
            vm((FFB, COVER), F32),
            dma(3),
            dma(2, NE), dma(2, NE),
            dma(NE), dma(NE),
            dma(4, 7), dma(4, 7),
            dma(2, 8), dma(2, 8),
            dma(2, 3), dma(2, 3),
            dma(2), dma(2),
            dma(15), dma(15),
            dma(6, NE), dma(6, NE),
            dma(2, NT), dma(2, NT),
            dma(NE), dma(NE),
            dma(4), dma(4),
            dma(2, NE),
        ],
        compiler_params=pltpu.CompilerParams(
            collective_id=0, has_side_effects=True, vmem_limit_bytes=60 * 1024 * 1024
        ),
    )(tokens, cotangent, ids, probs, dgate, dup, ddown, eg, eu, ed)


def finish_kernel(scale_expert, gtok, gdense, eact, erows, otok, ogate, oup, odown, eg, eu, ed):
    odd = lax.axis_index("ep") % 2

    @pl.when((pl.program_id(0) == 0) & (odd == 0))
    def _():
        for k, o in enumerate((ogate, oup, odown)):
            o[...] = gdense[k, :, 0:448]

    @pl.when((pl.program_id(0) == 0) & (odd == 1))
    def _():
        for k, o in enumerate((ogate, oup, odown)):
            o[...] = gdense[k, :, 64:512]

    otok[...] = gtok[...]
    for k, o in enumerate((eg, eu, ed)):
        o[...] = (dot_tn(eact[k], erows[k // 2]) * scale_expert).astype(BF16)


def finish(gtok, gdense, eact, erows, scale_expert):
    rows, width = gtok.shape
    step = 1024
    whole = lambda *shape: pl.BlockSpec(shape, lambda n: (0,) * len(shape))
    by_step = lambda *shape: pl.BlockSpec(shape + (step,), lambda n: (0,) * len(shape) + (n,))
    return pl.pallas_call(
        functools.partial(finish_kernel, scale_expert),
        name="finish",
        grid=(width // step,),
        in_specs=[by_step(rows), whole(3, FFB, COVER), whole(3, SLOTS, HID), by_step(2, SLOTS)],
        out_specs=[by_step(rows)] + [whole(FFB, 448)] * 3 + [by_step(HID)] * 3,
        out_shape=[jax.ShapeDtypeStruct((rows, width), BF16)]
        + [jax.ShapeDtypeStruct((FFB, 448), BF16)] * 3
        + [jax.ShapeDtypeStruct((HID, width), BF16)] * 3,
        compiler_params=pltpu.CompilerParams(vmem_limit_bytes=60 * 1024 * 1024),
    )(gtok, gdense, eact, erows)


def per_device(
    tokens, cotangent, route_ids, route_probs, dense_gate, dense_up, dense_down, expert_gate, expert_up, expert_down
):
    total_tokens = NE * GROUP
    scale_dense = 1.0 / math.sqrt(total_tokens)
    scale_expert = math.sqrt(NE * NT // 2 / (2.0 * total_tokens))
    gtok, gdense, eact, erows = exchange(
        tokens, cotangent, route_ids.T, route_probs.T, dense_gate.T, dense_up.T, dense_down,
        expert_gate[0], expert_up[0], expert_down[0], scale_dense,
    )
    gtok, ggate, gup, gdown, eg, eu, ed = finish(gtok, gdense, eact, erows, scale_expert)
    return (gtok, ggate.T, gup.T, gdown, eg[None], eu[None], ed[None])


def solution(mesh):
    return jax.shard_map(
        per_device,
        mesh=mesh,
        in_specs=(
            P(("ep", "tp"), None),
            P(("ep", "tp"), None),
            P("ep", None),
            P("ep", None),
            P("ep", "tp"),
            P("ep", "tp"),
            P("tp", "ep"),
            P(("ep", "tp"), None, None),
            P(("ep", "tp"), None, None),
            P(("ep", "tp"), None, None),
        ),
        out_specs=(
            P(("ep", "tp"), None),
            P("ep", "tp"),
            P("ep", "tp"),
            P("tp", "ep"),
            P(("ep", "tp"), None, None),
            P(("ep", "tp"), None, None),
            P(("ep", "tp"), None, None),
        ),
        check_vma=False,
    )
```

```python
import functools
import math

import jax
import jax.numpy as jnp
from jax import lax
from jax.experimental import pallas as pl
from jax.experimental.pallas import tpu as pltpu
from jax.sharding import PartitionSpec as P

MESH = pl.DeviceIdType.MESH
F32 = jnp.float32
BF16 = jnp.bfloat16

NE, NT = 16, 8
GROUP, CAP = 128, 6
SLOTS = NE * CAP
HALF_SLOTS = SLOTS // 2
COVER = 512
FFB = 304
HID = 192


def dot_nt(a, b):
    return lax.dot_general(a, b, (((1,), (1,)), ((), ())), preferred_element_type=F32)


def dot_nn(a, b):
    return lax.dot_general(a, b, (((1,), (0,)), ((), ())), preferred_element_type=F32)


def dot_tn(a, b):
    return lax.dot_general(a, b, (((0,), (0,)), ((), ())), preferred_element_type=F32)


def unit_grads(gate_pre, up_pre, d_hidden):
    sigmoid_gate = jax.nn.sigmoid(gate_pre)
    activated = gate_pre * sigmoid_gate
    hidden = (activated * up_pre).astype(BF16)
    d_gate = (d_hidden * up_pre * sigmoid_gate * (1.0 + gate_pre * (1.0 - sigmoid_gate))).astype(BF16)
    d_up = (d_hidden * activated).astype(BF16)
    return hidden, d_gate, d_up


def kernel(
    scale_dense,
    tok, cot, ids, probs, dgate, dup, ddown, eg, eu, ed,
    gtok, gdense, eact, erows,
    xy, route, rr, wt, wx, gx, part, c0r, x1r, x2r, z2r, hb, sel, sprob, ms, mr, we, eacc, bs, rb, dx, er, fs, fb, gacc,
    wsem, a_s, a_r, r_s, r_r, b_s, b_r, c0_s, c0_rs, c1_s, c1_rs, c2_s, c2_rs, d_s, d_r, m_s, m_r, e_s, e_r, f_s, f_r, k_s, k_r, osem,
):
    ep, tp = lax.axis_index("ep"), lax.axis_index("tp")
    x, zh, c = ep // 4, (ep // 2) % 2, ep % 2
    y, zl = tp // 2, tp % 2
    xo, xs, xr = (x + 2) % 4, (x + 1 + 2 * c) % 4, (x + 3 + 2 * c) % 4
    yo, ys, yr = (y + 2) % 4, (y + 1 + 2 * c) % 4, (y + 3 + 2 * c) % 4

    full, rest = slice(0, COVER), slice(128, COVER)

    def by_core(act):
        pl.when(c == 0)(lambda: act(full))
        pl.when(c == 1)(lambda: act(rest))

    def dev_x(xx):
        return ((xx * 2 + zh) * 2 + c, tp)

    def dev_y(yy):
        return (ep, yy * 2 + zl)

    dev_zh = ((x * 2 + 1 - zh) * 2 + c, tp)
    dev_core = ((x * 2 + zh) * 2 + 1 - c, tp)
    dev_zl = (ep, y * 2 + 1 - zl)

    def rc(src, dst, s, r, dev):
        return pltpu.make_async_remote_copy(
            src_ref=src, dst_ref=dst, send_sem=s, recv_sem=r, device_id=dev, device_id_type=MESH
        )

    def got(ref, r):
        rc(ref, ref, r, r, dev_core).wait_recv()

    def sent(ref, s):
        rc(ref, ref, s, s, dev_core).wait_send()

    def add(dst, srcs_):
        total = dst[...].astype(F32)
        for s in srcs_:
            total = total + s[...].astype(F32)
        dst[...] = total.astype(BF16)

    loads = [pltpu.make_async_copy(w, we.at[n], wsem.at[n]) for n, w in enumerate((eg, eu, ed))]
    for w in loads:
        w.start()

    @pl.when(c == 1)
    def _():
        rb[:, :, 0:128] = jnp.zeros((NE, SLOTS, 128), BF16)
        xy[:, :, :, :, :, 0:128] = jnp.zeros((2, NE, 4, 2, 16, 128), BF16)

    barrier = pltpu.get_barrier_semaphore()

    @pl.loop(1, NE)
    def _(k):
        pl.semaphore_signal(barrier, inc=1, device_id=((ep + k) % NE, tp), device_id_type=MESH)

    @pl.loop(1, NT)
    def _(k):
        pl.semaphore_signal(barrier, inc=1, device_id=(ep, (tp + k) % NT), device_id_type=MESH)


    pl.semaphore_wait(barrier, NE - 1 + NT - 1)

    srcs = (tok, cot)

    def a_copy(a, k):
        j = (ep + k) % NE
        at = pl.multiple_of(896 * (j // 2) + 512 * (j % 2), 128)
        return lambda lanes: rc(
            srcs[a].at[:, pl.ds(at, lanes.stop - lanes.start)],
            xy.at[a, ep, y, zl, :, lanes], a_s.at[a, k], a_r.at[a, k], (j, tp),
        )

    def a_send(a):
        @pl.loop(1, NE)
        def _(k):
            pl.when((ep + k) % 2 == 0)(lambda: a_copy(a, k)(full).start())
            pl.when((ep + k) % 2 == 1)(lambda: a_copy(a, k)(rest).start())

        @pl.when(c == 0)
        def _():
            xy[a, ep, y, zl] = srcs[a][:, pl.ds(pl.multiple_of(896 * (ep // 2), 128), 512)]

        @pl.when(c == 1)
        def _():
            xy[a, ep, y, zl, :, 128:512] = srcs[a][:, pl.ds(pl.multiple_of(896 * (ep // 2) + 512, 128), 384)]

    a_send(0)

    before = lax.broadcasted_iota(jnp.int32, (GROUP, GROUP), 0) < lax.broadcasted_iota(jnp.int32, (GROUP, GROUP), 1)
    across = [jnp.broadcast_to(ids[k : k + 1, :].astype(F32), (GROUP, GROUP)) for k in range(2)]
    down = [jnp.transpose(m) for m in across]
    codes = []
    for k in range(2):
        rank = jnp.zeros((1, GROUP), F32)
        for m in down:
            rank = rank + jnp.sum(jnp.where(before & (m == across[k]), 1.0, 0.0), axis=0, keepdims=True)
        idk = ids[k : k + 1, :]
        group_at = (ep % 8) * CAP
        fixed = (idk & 3) * (NE * HALF_SLOTS) + (idk >> 2) * HALF_SLOTS + group_at
        codes.append(fixed.astype(F32) + rank)
    route[...] = jnp.concatenate([codes[0], codes[1], probs[...], jnp.zeros((4, GROUP), F32)], axis=0)

    @pl.loop(1, NE)
    def _(k):
        rc(route, rr.at[ep], r_s.at[k], r_r.at[k], ((ep + k) % NE, tp)).start()

    a_send(1)
    def w_copy():
        return rc(wt.at[:, :, 0:128], wx, k_s.at[0], k_r.at[0], dev_core)

    def w_join():
        @pl.when(c == 0)
        def _():
            got(wx, k_r.at[0])
            for k in range(3):
                wt[k, :, 384:512] = wt[k, :, 384:512] + wx[k]

    blank = jnp.zeros((FFB, COVER - 448), BF16)

    @pl.when(c == 0)
    def _():
        for k, w in enumerate((dgate, dup, ddown)):
            wt[k] = jnp.concatenate([w[...], blank], axis=1)

    @pl.when(c == 1)
    def _():
        for k, w in enumerate((dgate, dup, ddown)):
            wt[k] = jnp.concatenate([blank, w[...]], axis=1)
        w_copy().start()

    rr[ep] = route[...]

    def got_a(a):
        @pl.loop(1, NE)
        def _(k):
            i = (ep + NE - k) % NE
            by_core(lambda lanes: got(xy.at[a, i, y, zl, :, lanes], a_r.at[a, k]))

    def send_b(a, h, n, yy, zz, dev):
        def act(lanes):
            ref = xy.at[a, 8 * h : 8 * h + 8, yy, zz, :, lanes]
            rc(ref, ref, b_s.at[2 * a + h, n], b_r.at[2 * a + h, n], dev).start()

        by_core(act)

    def got_b(a, h, n, yy, zz):
        by_core(lambda lanes: got(xy.at[a, 8 * h : 8 * h + 8, yy, zz, :, lanes], b_r.at[2 * a + h, n]))

    def sent_b(a, h, n):
        by_core(lambda lanes: sent(xy.at[a, 8 * h : 8 * h + 8, y, zl, :, lanes], b_s.at[2 * a + h, n]))

    def b_zero(a):
        for h in range(2):
            send_b(a, h, 0, y, zl, dev_zl)

    def b_first(a, h):
        send_b(a, h, 1, y, zl, dev_y(ys))
        send_b(a, h, 2, y, zl, dev_y(yr))

    def b_mid(a, h):
        got_b(a, h, 0, y, 1 - zl)
        send_b(a, h, 3, y, 1 - zl, dev_y(ys))
        send_b(a, h, 4, y, 1 - zl, dev_y(yr))

    def b_forward(a, h, second):
        if second:
            got_b(a, h, 3, yr, 1 - zl)
            send_b(a, h, 6, yr, 1 - zl, dev_y(ys))
        else:
            got_b(a, h, 1, yr, zl)
            send_b(a, h, 5, yr, zl, dev_y(ys))
            got_b(a, h, 2, ys, zl)

    def b_end(a, h):
        got_b(a, h, 5, yo, zl)
        got_b(a, h, 4, ys, 1 - zl)
        got_b(a, h, 6, yo, 1 - zl)

    def slots():
        @pl.loop(1, NE)
        def _(k):
            got(rr.at[(ep + NE - k) % NE], r_r.at[k])

        base = ((tp // 2) * (NE * HALF_SLOTS)).astype(F32)
        for h in range(2):
            sprob[h] = jnp.zeros((NE * HALF_SLOTS, 128), F32)

            @pl.loop(0, 8)
            def _(gl):
                row = rr[h * 8 + gl]
                numbers = lax.broadcasted_iota(jnp.int32, (NE * HALF_SLOTS, 128), 0).astype(F32)
                first = numbers == (row[0:1] - base)
                second = numbers == (row[1:2] - base)
                sel[h, :, pl.ds(pl.multiple_of(gl * 128, 128), 128)] = jnp.where(first | second, 1.0, 0.0).astype(BF16)
                sprob[h] += jnp.where(first, row[2:3], 0.0) + jnp.where(second, row[3:4], 0.0)

            sprob[h] = jnp.broadcast_to(jnp.sum(sprob[h], axis=1, keepdims=True), (NE * HALF_SLOTS, 128))

    spans = ((0, 2), (2, 3))

    def products(a):
        k0, k1 = spans[a]

        @pl.loop(0, 8)
        def _(p):
            def act(lanes):
                rows = xy[a, pl.ds(2 * p, 2), :, :, :, lanes].reshape(2 * GROUP, lanes.stop - lanes.start)
                for k in range(k0, k1):
                    res = dot_nt(wt[k, :, lanes], rows).astype(BF16)
                    part[2 * p, k] = res[:, :GROUP]
                    part[2 * p + 1, k] = res[:, GROUP:]

            by_core(act)
            rc(
                part.at[2 * p + 1 - c, k0:k1], c0r.at[p // 2, p % 2, k0:k1], c0_s.at[a, p], c0_rs.at[a, p], dev_core
            ).start()

    def sum_core(a):
        k0, k1 = spans[a]

        @pl.loop(0, 8)
        def _(p):
            got(c0r.at[p // 2, p % 2, k0:k1], c0_rs.at[a, p])
            for k in range(k0, k1):
                add(c0r.at[p // 2, p % 2, k], [part.at[2 * p + c, k]])

    def c1_sends(a):
        k0, k1 = spans[a]
        q = lambda xx: c0r.at[xx, :, k0:k1]
        return [
            rc(q(xo), x1r.at[:, k0:k1], c1_s.at[a, 0], c1_rs.at[a, 0], dev_x(xs)),
            rc(q(xr), x2r.at[1, :, k0:k1], c1_s.at[a, 1], c1_rs.at[a, 1], dev_x(xr)),
            rc(q(xs), x2r.at[0, :, k0:k1], c1_s.at[a, 2], c1_rs.at[a, 2], dev_x(xs)),
        ]

    def c1_first(a):
        for s in c1_sends(a)[:2]:
            s.start()

    def c1_second(a):
        k0, k1 = spans[a]
        sends = c1_sends(a)
        sends[0].wait_recv()
        for zz in range(2):
            for k in range(k0, k1):
                add(c0r.at[xs, zz, k], [x1r.at[zz, k]])
        sends[2].start()

    def c2_send(a):
        k0, k1 = spans[a]
        return rc(c0r.at[x, 1 - zh, k0:k1], z2r.at[k0:k1], c2_s.at[a], c2_rs.at[a], dev_zh)

    def c1_third(a):
        k0, k1 = spans[a]
        sends = c1_sends(a)
        for n in (1, 2):
            sends[n].wait_recv()
        for n, zz in enumerate((1 - zh, zh)):
            for k in range(k0, k1):
                add(c0r.at[x, zz, k], [x2r.at[0, zz, k], x2r.at[1, zz, k]])
            if n == 0:
                c2_send(a).start()

    def rows_of(h):
        return slice(HALF_SLOTS * h, HALF_SLOTS * (h + 1))

    def m_copy(a, h, j, lanes):
        return rc(
            ms.at[a, j, rows_of(h), lanes], mr.at[a, ep, rows_of(h), lanes], m_s.at[2 * a + h, j], m_r.at[2 * a + h, ep], (j, tp)
        )

    def routed(a, h):
        @pl.loop(0, 4)
        def _(n):
            jj = (x + n) % 4
            rows = xy[a, 8 * h : 8 * h + 8].reshape(8 * GROUP, COVER)
            at = pl.multiple_of(jj * 4 * HALF_SLOTS, 64)
            res = dot_nn(sel[h, pl.ds(at, 4 * HALF_SLOTS)], rows)
            if a == 1:
                res = res * sprob[h, pl.ds(at, 4 * HALF_SLOTS), 0:1]
            ms[a, pl.ds(jj * 4, 4), rows_of(h)] = res.astype(BF16).reshape(4, HALF_SLOTS, COVER)

            @pl.loop(0, 4)
            def _(m):
                j = jj * 4 + m

                @pl.when((j != ep) & (c == 0))
                def _():
                    m_copy(a, h, j, full).start()

                @pl.when((j != ep) & (c == 1))
                def _():
                    m_copy(a, h, j, rest).start()

                @pl.when(j == ep)
                def _():
                    mr[a, j, rows_of(h)] = ms[a, j, rows_of(h)]

    def got_routed(a, h):
        @pl.loop(0, 8)
        def _(p):
            @pl.when(2 * p != ep)
            def _():
                got(mr.at[a, 2 * p, rows_of(h)], m_r.at[2 * a + h, 2 * p])

            @pl.when(2 * p + 1 != ep)
            def _():
                got(mr.at[a, 2 * p + 1, rows_of(h), rest], m_r.at[2 * a + h, 2 * p + 1])

    def expert_forward(h):
        for a in range(2):
            got_routed(a, h)
        if h == 0:
            for w in loads:
                w.wait()
        for n, a in enumerate((0, 0, 1)):
            total = jnp.zeros((HALF_SLOTS, HID), F32)
            for p in range(8):
                total += dot_nt(mr[a, 2 * p, rows_of(h)], we[n, :, 896 * p : 896 * p + 512])
                total += dot_nt(mr[a, 2 * p + 1, rows_of(h), rest], we[n, :, 896 * p + 512 : 896 * p + 896])
            eacc[n] = total
        hidden, d_gate, d_up = unit_grads(eacc[0], eacc[1], eacc[2])
        eact[0, rows_of(h)] = d_gate
        eact[1, rows_of(h)] = d_up
        eact[2, rows_of(h)] = hidden

    def back_copy(h, i, lanes):
        return rc(bs.at[i, rows_of(h), lanes], rb.at[ep, rows_of(h), lanes], m_s.at[4 + h, i], m_r.at[4 + h, ep], (i, tp))

    def expert_back(h):
        @pl.loop(0, 8)
        def _(n):
            p = (ep // 2 + n) % 8
            g, u = eact[0, rows_of(h)], eact[1, rows_of(h)]
            for m, lanes in enumerate((full, rest)):
                i = 2 * p + m
                wide = pl.ds(pl.multiple_of(896 * p + 512 * m, 128), 512 - 128 * m)
                bs[i, rows_of(h), lanes] = (dot_nn(g, we[0, :, wide]) + dot_nn(u, we[1, :, wide])).astype(BF16)

                @pl.when(i != ep)
                def _():
                    back_copy(h, i, lanes).start()

                @pl.when(i == ep)
                def _():
                    rb[i, rows_of(h), lanes] = bs[i, rows_of(h), lanes]

    def got_back(h):
        @pl.loop(1, NE)
        def _(k):
            j = (ep + k) % NE

            @pl.when(c == 0)
            def _():
                got(rb.at[j, rows_of(h)], m_r.at[4 + h, j])

            @pl.when(c == 1)
            def _():
                got(rb.at[j, rows_of(h), rest], m_r.at[4 + h, j])

    def h_at(xx, zz):
        return hb.at[(xx * 2 + zz) * 2 + c]

    def send_d(n, xx, zz, dev):
        rc(h_at(xx, zz), h_at(xx, zz), d_s.at[n], d_r.at[n], dev).start()

    def got_d(n, xx, zz):
        got(h_at(xx, zz), d_r.at[n])

    def to_core(n, xx, zz):
        send_d(7 + n, xx, zz, dev_core)

    def d_first():
        for a in range(2):
            k0, k1 = spans[a]
            got(z2r.at[k0:k1], c2_rs.at[a])
        mine = [c0r[x, zh, k].astype(F32) + z2r[k].astype(F32) for k in range(3)]
        hidden, d_gate, d_up = unit_grads(*mine)
        hb[ep, 0] = d_gate
        hb[ep, 1] = d_up
        hb[ep, 2] = hidden
        send_d(0, x, zh, dev_zh)
        send_d(1, x, zh, dev_x(xs))
        send_d(2, x, zh, dev_x(xr))
        to_core(0, x, zh)

    def d_mid():
        got_d(0, x, 1 - zh)
        send_d(3, x, 1 - zh, dev_x(xs))
        send_d(4, x, 1 - zh, dev_x(xr))
        to_core(1, x, 1 - zh)

    def d_forward():
        got_d(1, xr, zh)
        send_d(5, xr, zh, dev_x(xs))
        to_core(2, xr, zh)
        got_d(3, xr, 1 - zh)
        send_d(6, xr, 1 - zh, dev_x(xs))
        to_core(3, xr, 1 - zh)

    def d_sides():
        got_d(2, xs, zh)
        to_core(4, xs, zh)
        got_d(4, xs, 1 - zh)
        to_core(5, xs, 1 - zh)

    def d_far():
        got_d(5, xo, zh)
        to_core(6, xo, zh)
        got_d(6, xo, 1 - zh)
        to_core(7, xo, 1 - zh)

    def d_core(n, xx):
        got(hb.at[(xx * 2 + zh) * 2 + 1 - c], d_r.at[7 + n])
        got(hb.at[(xx * 2 + 1 - zh) * 2 + 1 - c], d_r.at[8 + n])

    def input_grads(xx):
        h = xx // 2

        @pl.loop(0, 2)
        def _(n):
            g = 4 * xx + 2 * n
            back = rb[:, pl.ds(pl.multiple_of(HALF_SLOTS * h, 16), HALF_SLOTS)].reshape(NE * HALF_SLOTS, COVER)
            at = pl.multiple_of((xx % 2) * 512 + n * 256, 256)
            total = dot_tn(sel[h, :, pl.ds(at, 256)], back)
            for k in range(2):
                both = jnp.concatenate([hb[g, k], hb[g + 1, k]], axis=1)
                total = total + dot_tn(both, wt[k])
            dx[pl.ds(g, 2)] = total.astype(BF16).reshape(2, 4, 2, 16, COVER)

    def e_copy(xx, t, lanes):
        src = dx.at[pl.ds(4 * xx, 4), t // 2, t % 2, :, lanes]
        return rc(src, er.at[xx, tp, :, :, lanes], e_s.at[xx, t], e_r.at[xx, tp], (ep, t))

    def e_start(xx):
        @pl.loop(1, NT)
        def _(k):
            by_core(lambda lanes: e_copy(xx, (tp + k) % NT, lanes).start())

    def f_copy(j, lanes):
        return rc(fs.at[j, :, lanes], fb.at[ep, :, lanes], f_s.at[j], f_r.at[ep], (j, tp))

    def e_last(xx):
        @pl.loop(1, NT)
        def _(k):
            t = (tp + k) % NT
            by_core(lambda lanes: got(er.at[xx, t, :, :, lanes], e_r.at[xx, t]))

        er[xx, tp] = dx[pl.ds(4 * xx, 4), y, zl]
        total = er[xx, 0].astype(F32)
        for t in range(1, NT):
            total = total + er[xx, t].astype(F32)
        fs[pl.ds(4 * xx, 4)] = total.astype(BF16)

        @pl.loop(0, 4)
        def _(n):
            j = 4 * xx + (ep + n) % 4

            @pl.when(j != ep)
            def _():
                by_core(lambda lanes: f_copy(j, lanes).start())

            @pl.when(j == ep)
            def _():
                fb[j] = fs[j]

    def g_copy():
        return rc(gdense.at[:, :, 384:512], gx, k_s.at[1], k_r.at[1], dev_core)

    def weight_grads(k):
        gacc[...] = jnp.zeros((FFB, COVER), F32)

        @pl.loop(0, 4)
        def _(n):
            left = jnp.concatenate([hb[4 * n + m, k] for m in range(4)], axis=1)
            rows = xy[0 if k < 2 else 1, pl.ds(4 * n, 4)].reshape(4 * GROUP, COVER)
            gacc[...] += dot_nn(left, rows)

        gdense[k] = (gacc[...] * scale_dense).astype(BF16)
        if k == 2:
            pl.when(c == 0)(lambda: g_copy().start())

    got_a(0)
    b_zero(0)
    b_first(0, 0)
    b_first(0, 1)
    got_a(1)
    b_zero(1)
    slots()
    b_mid(0, 0)
    b_forward(0, 0, False)
    b_forward(0, 0, True)
    b_mid(0, 1)
    b_first(1, 0)
    b_forward(0, 1, False)
    b_end(0, 0)
    routed(0, 0)
    b_forward(0, 1, True)
    b_mid(1, 0)
    b_first(1, 1)
    b_end(0, 1)
    w_join()
    products(0)
    b_forward(1, 0, False)
    sum_core(0)
    c1_first(0)
    b_forward(1, 0, True)
    routed(0, 1)
    b_mid(1, 1)
    b_forward(1, 1, False)
    c1_second(0)
    b_end(1, 0)
    routed(1, 0)
    b_forward(1, 1, True)
    c1_third(0)
    b_end(1, 1)
    routed(1, 1)
    products(1)
    sum_core(1)
    c1_first(1)
    expert_forward(0)
    c1_second(1)
    expert_back(0)
    c1_third(1)
    d_first()
    expert_forward(1)
    expert_back(1)
    d_mid()
    d_forward()

    outs = []
    for a in range(2):
        for p in range(8):
            for m, lanes in enumerate((full, rest)):
                at = 896 * p + 512 * m
                outs.append(
                    pltpu.make_async_copy(
                        mr.at[a, 2 * p + m, :, lanes], erows.at[a, :, at : at + 512 - 128 * m], osem.at[a, 2 * p + m]
                    )
                )
    for o in outs:
        o.start()

    d_sides()
    d_core(0, x)
    got_back(0)
    got_back(1)
    input_grads(x)
    e_start(x)
    d_core(2, xs)
    d_core(4, xr)
    input_grads(xr)
    e_start(xr)
    d_far()
    input_grads(xs)
    e_start(xs)
    d_core(6, xo)
    input_grads(xo)
    e_start(xo)
    weight_grads(0)
    e_last(x)
    weight_grads(1)
    e_last(xr)
    weight_grads(2)
    e_last(xs)
    e_last(xo)

    @pl.loop(1, NE)
    def _(k):
        i = (ep + k) % NE
        pl.when(i % 2 == 0)(lambda: got(fb.at[i], f_r.at[i]))
        pl.when(i % 2 == 1)(lambda: got(fb.at[i, :, rest], f_r.at[i]))

    for p in range(8):
        for m, lanes in enumerate((full, rest)):
            at = slice(896 * p + 512 * m, 896 * p + 512 + 384 * m)
            gtok[:, at] = (cot[:, at].astype(F32) + fb[2 * p + m, :, lanes].astype(F32)).astype(BF16)

    @pl.when(c == 1)
    def _():
        got(gx, k_r.at[1])
        gdense[:, :, 0:128] = gx[...]

    for o in outs:
        o.wait()

    @pl.loop(1, NE)
    def _(k):
        j = (ep + k) % NE
        for a in range(2):
            pl.when(j % 2 == 0)(lambda: a_copy(a, k)(full).wait_send())
            pl.when(j % 2 == 1)(lambda: a_copy(a, k)(rest).wait_send())
        sent(route, r_s.at[k])
        by_core(lambda lanes: f_copy(j, lanes).wait_send())
        for h in range(2):
            for a in range(2):

                @pl.when(c == 0)
                def _():
                    m_copy(a, h, j, full).wait_send()

                @pl.when(c == 1)
                def _():
                    m_copy(a, h, j, rest).wait_send()

            @pl.when(j % 2 == 0)
            def _():
                back_copy(h, j, full).wait_send()

            @pl.when(j % 2 == 1)
            def _():
                back_copy(h, j, rest).wait_send()

    for a in range(2):
        for h in range(2):
            for n in range(7):
                sent_b(a, h, n)

        k0, k1 = spans[a]

        @pl.loop(0, 8)
        def _(p):
            sent(c0r.at[p // 2, p % 2, k0:k1], c0_s.at[a, p])

        for s in c1_sends(a):
            s.wait_send()
        c2_send(a).wait_send()

    @pl.loop(0, 15)
    def _(n):
        sent(h_at(x, zh), d_s.at[n])

    @pl.loop(1, NT)
    def _(k):
        for n in range(4):
            by_core(lambda lanes: e_copy(n, (tp + k) % NT, lanes).wait_send())

    @pl.when(c == 0)
    def _():
        g_copy().wait_send()

    @pl.when(c == 1)
    def _():
        w_copy().wait_send()


def exchange(tokens, cotangent, ids, probs, dgate, dup, ddown, eg, eu, ed, scale_dense):
    vm = lambda shape, dt=BF16: pltpu.VMEM(shape, dt)
    dma = lambda *shape: pltpu.SemaphoreType.DMA(shape)
    width = tokens.shape[1]
    vspec = pl.BlockSpec(memory_space=pltpu.VMEM)
    hspec = pl.BlockSpec(memory_space=pl.ANY)
    return pl.pallas_call(
        functools.partial(kernel, scale_dense),
        name="exchange",
        out_shape=(
            jax.ShapeDtypeStruct(tokens.shape, BF16),
            jax.ShapeDtypeStruct((3, FFB, COVER), BF16),
            jax.ShapeDtypeStruct((3, SLOTS, HID), BF16),
            jax.ShapeDtypeStruct((2, SLOTS, width), BF16),
        ),
        in_specs=[vspec] * 7 + [hspec] * 3,
        out_specs=(vspec, vspec, vspec, hspec),
        scratch_shapes=[
            vm((2, NE, 4, 2, 16, COVER)),
            vm((8, GROUP), F32),
            vm((NE, 8, GROUP), F32),
            vm((3, FFB, COVER)),
            vm((3, FFB, 128)),
            vm((3, FFB, 128)),
            vm((NE, 3, FFB, GROUP)),
            vm((4, 2, 3, FFB, GROUP)),
            vm((2, 3, FFB, GROUP)),
            vm((2, 2, 3, FFB, GROUP)),
            vm((3, FFB, GROUP)),
            vm((NE, 3, FFB, GROUP)),
            vm((2, NE * HALF_SLOTS, 8 * GROUP)),
            vm((2, NE * HALF_SLOTS, 128), F32),
            vm((2, NE, SLOTS, COVER)),
            vm((2, NE, SLOTS, COVER)),
            vm((3, HID, width)),
            vm((3, HALF_SLOTS, HID), F32),
            vm((NE, SLOTS, COVER)),
            vm((NE, SLOTS, COVER)),
            vm((NE, 4, 2, 16, COVER)),
            vm((4, NT, 4, 16, COVER)),
            vm((NE, 16, COVER)),
            vm((NE, 16, COVER)),
            vm((FFB, COVER), F32),
            dma(3),
            dma(2, NE), dma(2, NE),
            dma(NE), dma(NE),
            dma(4, 7), dma(4, 7),
            dma(2, 8), dma(2, 8),
            dma(2, 3), dma(2, 3),
            dma(2), dma(2),
            dma(15), dma(15),
            dma(6, NE), dma(6, NE),
            dma(4, NT), dma(4, NT),
            dma(NE), dma(NE),
            dma(2), dma(2),
            dma(2, NE),
        ],
        compiler_params=pltpu.CompilerParams(
            collective_id=0, has_side_effects=True, vmem_limit_bytes=60 * 1024 * 1024
        ),
    )(tokens, cotangent, ids, probs, dgate, dup, ddown, eg, eu, ed)


def finish_kernel(scale_expert, gtok, gdense, eact, erows, otok, ogate, oup, odown, eg, eu, ed):
    odd = lax.axis_index("ep") % 2

    @pl.when((pl.program_id(0) == 0) & (odd == 0))
    def _():
        for k, o in enumerate((ogate, oup, odown)):
            o[...] = gdense[k, :, 0:448]

    @pl.when((pl.program_id(0) == 0) & (odd == 1))
    def _():
        for k, o in enumerate((ogate, oup, odown)):
            o[...] = gdense[k, :, 64:512]

    otok[...] = gtok[...]
    for k, o in enumerate((eg, eu, ed)):
        o[...] = (dot_tn(eact[k], erows[k // 2]) * scale_expert).astype(BF16)


def finish(gtok, gdense, eact, erows, scale_expert):
    rows, width = gtok.shape
    step = 1024
    whole = lambda *shape: pl.BlockSpec(shape, lambda n: (0,) * len(shape))
    by_step = lambda *shape: pl.BlockSpec(shape + (step,), lambda n: (0,) * len(shape) + (n,))
    return pl.pallas_call(
        functools.partial(finish_kernel, scale_expert),
        name="finish",
        grid=(width // step,),
        in_specs=[by_step(rows), whole(3, FFB, COVER), whole(3, SLOTS, HID), by_step(2, SLOTS)],
        out_specs=[by_step(rows)] + [whole(FFB, 448)] * 3 + [by_step(HID)] * 3,
        out_shape=[jax.ShapeDtypeStruct((rows, width), BF16)]
        + [jax.ShapeDtypeStruct((FFB, 448), BF16)] * 3
        + [jax.ShapeDtypeStruct((HID, width), BF16)] * 3,
        compiler_params=pltpu.CompilerParams(vmem_limit_bytes=60 * 1024 * 1024),
    )(gtok, gdense, eact, erows)


def per_device(
    tokens, cotangent, route_ids, route_probs, dense_gate, dense_up, dense_down, expert_gate, expert_up, expert_down
):
    total_tokens = NE * GROUP
    scale_dense = 1.0 / math.sqrt(total_tokens)
    scale_expert = math.sqrt(NE * NT // 2 / (2.0 * total_tokens))
    gtok, gdense, eact, erows = exchange(
        tokens, cotangent, route_ids.T, route_probs.T, dense_gate.T, dense_up.T, dense_down,
        expert_gate[0], expert_up[0], expert_down[0], scale_dense,
    )
    gtok, ggate, gup, gdown, eg, eu, ed = finish(gtok, gdense, eact, erows, scale_expert)
    return (gtok, ggate.T, gup.T, gdown, eg[None], eu[None], ed[None])


def solution(mesh):
    return jax.shard_map(
        per_device,
        mesh=mesh,
        in_specs=(
            P(("ep", "tp"), None),
            P(("ep", "tp"), None),
            P("ep", None),
            P("ep", None),
            P("ep", "tp"),
            P("ep", "tp"),
            P("tp", "ep"),
            P(("ep", "tp"), None, None),
            P(("ep", "tp"), None, None),
            P(("ep", "tp"), None, None),
        ),
        out_specs=(
            P(("ep", "tp"), None),
            P("ep", "tp"),
            P("ep", "tp"),
            P("tp", "ep"),
            P(("ep", "tp"), None, None),
            P(("ep", "tp"), None, None),
            P(("ep", "tp"), None, None),
        ),
        check_vma=False,
    )
```

```python
import functools
import math

import jax
import jax.numpy as jnp
from jax import lax
from jax.experimental import pallas as pl
from jax.experimental.pallas import tpu as pltpu
from jax.sharding import PartitionSpec as P

MESH = pl.DeviceIdType.MESH
F32 = jnp.float32
BF16 = jnp.bfloat16

NE, NT = 16, 8
GROUP, CAP = 128, 6
SLOTS = NE * CAP
HALF_SLOTS = SLOTS // 2
COVER = 512
FFB = 304
HID = 192


def dot_nt(a, b):
    return lax.dot_general(a, b, (((1,), (1,)), ((), ())), preferred_element_type=F32)


def dot_nn(a, b):
    return lax.dot_general(a, b, (((1,), (0,)), ((), ())), preferred_element_type=F32)


def dot_tn(a, b):
    return lax.dot_general(a, b, (((0,), (0,)), ((), ())), preferred_element_type=F32)


def unit_grads(gate_pre, up_pre, d_hidden):
    sigmoid_gate = jax.nn.sigmoid(gate_pre)
    activated = gate_pre * sigmoid_gate
    hidden = (activated * up_pre).astype(BF16)
    d_gate = (d_hidden * up_pre * sigmoid_gate * (1.0 + gate_pre * (1.0 - sigmoid_gate))).astype(BF16)
    d_up = (d_hidden * activated).astype(BF16)
    return hidden, d_gate, d_up


def kernel(
    scale_dense,
    tok, cot, ids, probs, dgate, dup, ddown, eg, eu, ed,
    gtok, gdense, eact, erows,
    xy, route, rr, wt, wx, gx, part, c0r, x1r, x2r, z2r, hb, sel, sprob, ms, mr, we, eacc, bs, rb, dx, er, fs, fb, gacc,
    wsem, a_s, a_r, r_s, r_r, b_s, b_r, c0_s, c0_rs, c1_s, c1_rs, c2_s, c2_rs, d_s, d_r, m_s, m_r, e_s, e_r, f_s, f_r, k_s, k_r, osem,
):
    ep, tp = lax.axis_index("ep"), lax.axis_index("tp")
    x, zh, c = ep // 4, (ep // 2) % 2, ep % 2
    y, zl = tp // 2, tp % 2
    xo, xs, xr = (x + 2) % 4, (x + 1 + 2 * c) % 4, (x + 3 + 2 * c) % 4
    yo, ys, yr = (y + 2) % 4, (y + 1 + 2 * c) % 4, (y + 3 + 2 * c) % 4

    full, rest = slice(0, COVER), slice(128, COVER)

    def by_core(act):
        pl.when(c == 0)(lambda: act(full))
        pl.when(c == 1)(lambda: act(rest))

    def dev_x(xx):
        return ((xx * 2 + zh) * 2 + c, tp)

    def dev_y(yy):
        return (ep, yy * 2 + zl)

    dev_zh = ((x * 2 + 1 - zh) * 2 + c, tp)
    dev_core = ((x * 2 + zh) * 2 + 1 - c, tp)
    dev_zl = (ep, y * 2 + 1 - zl)

    def rc(src, dst, s, r, dev):
        return pltpu.make_async_remote_copy(
            src_ref=src, dst_ref=dst, send_sem=s, recv_sem=r, device_id=dev, device_id_type=MESH
        )

    def got(ref, r):
        rc(ref, ref, r, r, dev_core).wait_recv()

    def sent(ref, s):
        rc(ref, ref, s, s, dev_core).wait_send()

    def add(dst, srcs_):
        total = dst[...].astype(F32)
        for s in srcs_:
            total = total + s[...].astype(F32)
        dst[...] = total.astype(BF16)

    loads = [pltpu.make_async_copy(w, we.at[n], wsem.at[n]) for n, w in enumerate((eg, eu, ed))]
    for w in loads:
        w.start()

    @pl.when(c == 1)
    def _():
        rb[:, :, 0:128] = jnp.zeros((NE, SLOTS, 128), BF16)
        xy[:, :, :, :, :, 0:128] = jnp.zeros((2, NE, 4, 2, 16, 128), BF16)

    barrier = pltpu.get_barrier_semaphore()

    @pl.loop(1, NE)
    def _(k):
        pl.semaphore_signal(barrier, inc=1, device_id=((ep + k) % NE, tp), device_id_type=MESH)

    @pl.loop(1, NT)
    def _(k):
        pl.semaphore_signal(barrier, inc=1, device_id=(ep, (tp + k) % NT), device_id_type=MESH)


    pl.semaphore_wait(barrier, NE - 1 + NT - 1)

    srcs = (tok, cot)

    def a_copy(a, k):
        j = (ep + k) % NE
        at = pl.multiple_of(896 * (j // 2) + 512 * (j % 2), 128)
        return lambda lanes: rc(
            srcs[a].at[:, pl.ds(at, lanes.stop - lanes.start)],
            xy.at[a, ep, y, zl, :, lanes], a_s.at[a, k], a_r.at[a, k], (j, tp),
        )

    def a_send(a):
        @pl.loop(1, NE)
        def _(k):
            pl.when((ep + k) % 2 == 0)(lambda: a_copy(a, k)(full).start())
            pl.when((ep + k) % 2 == 1)(lambda: a_copy(a, k)(rest).start())

        @pl.when(c == 0)
        def _():
            xy[a, ep, y, zl] = srcs[a][:, pl.ds(pl.multiple_of(896 * (ep // 2), 128), 512)]

        @pl.when(c == 1)
        def _():
            xy[a, ep, y, zl, :, 128:512] = srcs[a][:, pl.ds(pl.multiple_of(896 * (ep // 2) + 512, 128), 384)]

    a_send(0)

    before = lax.broadcasted_iota(jnp.int32, (GROUP, GROUP), 0) < lax.broadcasted_iota(jnp.int32, (GROUP, GROUP), 1)
    across = [jnp.broadcast_to(ids[k : k + 1, :].astype(F32), (GROUP, GROUP)) for k in range(2)]
    down = [jnp.transpose(m) for m in across]
    codes = []
    for k in range(2):
        rank = jnp.zeros((1, GROUP), F32)
        for m in down:
            rank = rank + jnp.sum(jnp.where(before & (m == across[k]), 1.0, 0.0), axis=0, keepdims=True)
        idk = ids[k : k + 1, :]
        group_at = (ep % 8) * CAP
        fixed = (idk & 3) * (NE * HALF_SLOTS) + (idk >> 2) * HALF_SLOTS + group_at
        codes.append(fixed.astype(F32) + rank)
    route[...] = jnp.concatenate([codes[0], codes[1], probs[...], jnp.zeros((4, GROUP), F32)], axis=0)

    @pl.loop(1, NE)
    def _(k):
        rc(route, rr.at[ep], r_s.at[k], r_r.at[k], ((ep + k) % NE, tp)).start()

    a_send(1)
    def w_copy():
        return rc(wt.at[:, :, 0:128], wx, k_s.at[0], k_r.at[0], dev_core)

    def w_join():
        @pl.when(c == 0)
        def _():
            got(wx, k_r.at[0])
            for k in range(3):
                wt[k, :, 384:512] = wt[k, :, 384:512] + wx[k]

    blank = jnp.zeros((FFB, COVER - 448), BF16)

    @pl.when(c == 0)
    def _():
        for k, w in enumerate((dgate, dup, ddown)):
            wt[k] = jnp.concatenate([w[...], blank], axis=1)

    @pl.when(c == 1)
    def _():
        for k, w in enumerate((dgate, dup, ddown)):
            wt[k] = jnp.concatenate([blank, w[...]], axis=1)
        w_copy().start()

    rr[ep] = route[...]

    def got_a(a):
        @pl.loop(1, NE)
        def _(k):
            i = (ep + NE - k) % NE
            by_core(lambda lanes: got(xy.at[a, i, y, zl, :, lanes], a_r.at[a, k]))

    def send_b(a, h, n, yy, zz, dev):
        def act(lanes):
            ref = xy.at[a, 8 * h : 8 * h + 8, yy, zz, :, lanes]
            rc(ref, ref, b_s.at[2 * a + h, n], b_r.at[2 * a + h, n], dev).start()

        by_core(act)

    def got_b(a, h, n, yy, zz):
        by_core(lambda lanes: got(xy.at[a, 8 * h : 8 * h + 8, yy, zz, :, lanes], b_r.at[2 * a + h, n]))

    def sent_b(a, h, n):
        by_core(lambda lanes: sent(xy.at[a, 8 * h : 8 * h + 8, y, zl, :, lanes], b_s.at[2 * a + h, n]))

    def b_zero(a):
        for h in range(2):
            send_b(a, h, 0, y, zl, dev_zl)

    def b_first(a, h):
        send_b(a, h, 1, y, zl, dev_y(ys))
        send_b(a, h, 2, y, zl, dev_y(yr))

    def b_mid(a, h):
        got_b(a, h, 0, y, 1 - zl)
        send_b(a, h, 3, y, 1 - zl, dev_y(ys))
        send_b(a, h, 4, y, 1 - zl, dev_y(yr))

    def b_forward(a, h, second):
        if second:
            got_b(a, h, 3, yr, 1 - zl)
            send_b(a, h, 6, yr, 1 - zl, dev_y(ys))
        else:
            got_b(a, h, 1, yr, zl)
            send_b(a, h, 5, yr, zl, dev_y(ys))
            got_b(a, h, 2, ys, zl)

    def b_end(a, h):
        got_b(a, h, 5, yo, zl)
        got_b(a, h, 4, ys, 1 - zl)
        got_b(a, h, 6, yo, 1 - zl)

    def slots():
        @pl.loop(1, NE)
        def _(k):
            got(rr.at[(ep + NE - k) % NE], r_r.at[k])

        base = ((tp // 2) * (NE * HALF_SLOTS)).astype(F32)
        for h in range(2):
            sprob[h] = jnp.zeros((NE * HALF_SLOTS, 128), F32)

            @pl.loop(0, 8)
            def _(gl):
                row = rr[h * 8 + gl]
                numbers = lax.broadcasted_iota(jnp.int32, (NE * HALF_SLOTS, 128), 0).astype(F32)
                first = numbers == (row[0:1] - base)
                second = numbers == (row[1:2] - base)
                sel[h, :, pl.ds(pl.multiple_of(gl * 128, 128), 128)] = jnp.where(first | second, 1.0, 0.0).astype(BF16)
                sprob[h] += jnp.where(first, row[2:3], 0.0) + jnp.where(second, row[3:4], 0.0)

            sprob[h] = jnp.broadcast_to(jnp.sum(sprob[h], axis=1, keepdims=True), (NE * HALF_SLOTS, 128))

    spans = ((0, 2), (2, 3))

    def products(a):
        k0, k1 = spans[a]

        @pl.loop(0, 8)
        def _(p):
            def act(lanes):
                rows = xy[a, pl.ds(2 * p, 2), :, :, :, lanes].reshape(2 * GROUP, lanes.stop - lanes.start)
                for k in range(k0, k1):
                    res = dot_nt(wt[k, :, lanes], rows).astype(BF16)
                    part[2 * p, k] = res[:, :GROUP]
                    part[2 * p + 1, k] = res[:, GROUP:]

            by_core(act)
            rc(
                part.at[2 * p + 1 - c, k0:k1], c0r.at[p // 2, p % 2, k0:k1], c0_s.at[a, p], c0_rs.at[a, p], dev_core
            ).start()

    def sum_core(a):
        k0, k1 = spans[a]

        @pl.loop(0, 8)
        def _(p):
            got(c0r.at[p // 2, p % 2, k0:k1], c0_rs.at[a, p])
            for k in range(k0, k1):
                add(c0r.at[p // 2, p % 2, k], [part.at[2 * p + c, k]])

    def c1_sends(a):
        k0, k1 = spans[a]
        q = lambda xx: c0r.at[xx, :, k0:k1]
        return [
            rc(q(xo), x1r.at[:, k0:k1], c1_s.at[a, 0], c1_rs.at[a, 0], dev_x(xs)),
            rc(q(xr), x2r.at[1, :, k0:k1], c1_s.at[a, 1], c1_rs.at[a, 1], dev_x(xr)),
            rc(q(xs), x2r.at[0, :, k0:k1], c1_s.at[a, 2], c1_rs.at[a, 2], dev_x(xs)),
        ]

    def c1_first(a):
        for s in c1_sends(a)[:2]:
            s.start()

    def c1_second(a):
        k0, k1 = spans[a]
        sends = c1_sends(a)
        sends[0].wait_recv()
        for zz in range(2):
            for k in range(k0, k1):
                add(c0r.at[xs, zz, k], [x1r.at[zz, k]])
        sends[2].start()

    def c2_send(a):
        k0, k1 = spans[a]
        return rc(c0r.at[x, 1 - zh, k0:k1], z2r.at[k0:k1], c2_s.at[a], c2_rs.at[a], dev_zh)

    def c1_third(a):
        k0, k1 = spans[a]
        sends = c1_sends(a)
        for n in (1, 2):
            sends[n].wait_recv()
        for n, zz in enumerate((1 - zh, zh)):
            for k in range(k0, k1):
                add(c0r.at[x, zz, k], [x2r.at[0, zz, k], x2r.at[1, zz, k]])
            if n == 0:
                c2_send(a).start()

    def rows_of(h):
        return slice(HALF_SLOTS * h, HALF_SLOTS * (h + 1))

    def m_copy(a, h, j, lanes):
        return rc(
            ms.at[a, j, rows_of(h), lanes], mr.at[a, ep, rows_of(h), lanes], m_s.at[2 * a + h, j], m_r.at[2 * a + h, ep], (j, tp)
        )

    def routed(a, h):
        @pl.loop(0, 4)
        def _(n):
            jj = (x + n) % 4
            rows = xy[a, 8 * h : 8 * h + 8].reshape(8 * GROUP, COVER)
            at = pl.multiple_of(jj * 4 * HALF_SLOTS, 64)
            res = dot_nn(sel[h, pl.ds(at, 4 * HALF_SLOTS)], rows)
            if a == 1:
                res = res * sprob[h, pl.ds(at, 4 * HALF_SLOTS), 0:1]
            ms[a, pl.ds(jj * 4, 4), rows_of(h)] = res.astype(BF16).reshape(4, HALF_SLOTS, COVER)

            @pl.loop(0, 4)
            def _(m):
                j = jj * 4 + m

                @pl.when((j != ep) & (c == 0))
                def _():
                    m_copy(a, h, j, full).start()

                @pl.when((j != ep) & (c == 1))
                def _():
                    m_copy(a, h, j, rest).start()

                @pl.when(j == ep)
                def _():
                    mr[a, j, rows_of(h)] = ms[a, j, rows_of(h)]

    def got_routed(a, h):
        @pl.loop(0, 8)
        def _(p):
            @pl.when(2 * p != ep)
            def _():
                got(mr.at[a, 2 * p, rows_of(h)], m_r.at[2 * a + h, 2 * p])

            @pl.when(2 * p + 1 != ep)
            def _():
                got(mr.at[a, 2 * p + 1, rows_of(h), rest], m_r.at[2 * a + h, 2 * p + 1])

    def expert_forward(h):
        for a in range(2):
            got_routed(a, h)
        if h == 0:
            for w in loads:
                w.wait()
        for n, a in enumerate((0, 0, 1)):
            total = jnp.zeros((HALF_SLOTS, HID), F32)
            for p in range(8):
                total += dot_nt(mr[a, 2 * p, rows_of(h)], we[n, :, 896 * p : 896 * p + 512])
                total += dot_nt(mr[a, 2 * p + 1, rows_of(h), rest], we[n, :, 896 * p + 512 : 896 * p + 896])
            eacc[n] = total
        hidden, d_gate, d_up = unit_grads(eacc[0], eacc[1], eacc[2])
        eact[0, rows_of(h)] = d_gate
        eact[1, rows_of(h)] = d_up
        eact[2, rows_of(h)] = hidden

    def back_copy(h, i, lanes):
        return rc(bs.at[i, rows_of(h), lanes], rb.at[ep, rows_of(h), lanes], m_s.at[4 + h, i], m_r.at[4 + h, ep], (i, tp))

    def expert_back(h):
        @pl.loop(0, 8)
        def _(n):
            p = (ep // 2 + n) % 8
            g, u = eact[0, rows_of(h)], eact[1, rows_of(h)]
            for m, lanes in enumerate((full, rest)):
                i = 2 * p + m
                wide = pl.ds(pl.multiple_of(896 * p + 512 * m, 128), 512 - 128 * m)
                bs[i, rows_of(h), lanes] = (dot_nn(g, we[0, :, wide]) + dot_nn(u, we[1, :, wide])).astype(BF16)

                @pl.when(i != ep)
                def _():
                    back_copy(h, i, lanes).start()

                @pl.when(i == ep)
                def _():
                    rb[i, rows_of(h), lanes] = bs[i, rows_of(h), lanes]

    def got_back(h):
        @pl.loop(1, NE)
        def _(k):
            j = (ep + k) % NE

            @pl.when(c == 0)
            def _():
                got(rb.at[j, rows_of(h)], m_r.at[4 + h, j])

            @pl.when(c == 1)
            def _():
                got(rb.at[j, rows_of(h), rest], m_r.at[4 + h, j])

    def h_at(xx, zz):
        return hb.at[(xx * 2 + zz) * 2 + c]

    def send_d(n, xx, zz, dev):
        rc(h_at(xx, zz), h_at(xx, zz), d_s.at[n], d_r.at[n], dev).start()

    def got_d(n, xx, zz):
        got(h_at(xx, zz), d_r.at[n])

    def to_core(n, xx, zz):
        send_d(7 + n, xx, zz, dev_core)

    def d_first():
        for a in range(2):
            k0, k1 = spans[a]
            got(z2r.at[k0:k1], c2_rs.at[a])
        mine = [c0r[x, zh, k].astype(F32) + z2r[k].astype(F32) for k in range(3)]
        hidden, d_gate, d_up = unit_grads(*mine)
        hb[ep, 0] = d_gate
        hb[ep, 1] = d_up
        hb[ep, 2] = hidden
        send_d(0, x, zh, dev_zh)
        send_d(1, x, zh, dev_x(xs))
        send_d(2, x, zh, dev_x(xr))
        to_core(0, x, zh)

    def d_mid():
        got_d(0, x, 1 - zh)
        send_d(3, x, 1 - zh, dev_x(xs))
        send_d(4, x, 1 - zh, dev_x(xr))
        to_core(1, x, 1 - zh)

    def d_forward():
        got_d(1, xr, zh)
        send_d(5, xr, zh, dev_x(xs))
        to_core(2, xr, zh)
        got_d(3, xr, 1 - zh)
        send_d(6, xr, 1 - zh, dev_x(xs))
        to_core(3, xr, 1 - zh)

    def d_sides():
        got_d(2, xs, zh)
        to_core(4, xs, zh)
        got_d(4, xs, 1 - zh)
        to_core(5, xs, 1 - zh)

    def d_far():
        got_d(5, xo, zh)
        to_core(6, xo, zh)
        got_d(6, xo, 1 - zh)
        to_core(7, xo, 1 - zh)

    def d_core(n, xx):
        got(hb.at[(xx * 2 + zh) * 2 + 1 - c], d_r.at[7 + n])
        got(hb.at[(xx * 2 + 1 - zh) * 2 + 1 - c], d_r.at[8 + n])

    def input_grads(xx):
        h = xx // 2

        @pl.loop(0, 2)
        def _(n):
            g = 4 * xx + 2 * n
            back = rb[:, pl.ds(pl.multiple_of(HALF_SLOTS * h, 16), HALF_SLOTS)].reshape(NE * HALF_SLOTS, COVER)
            at = pl.multiple_of((xx % 2) * 512 + n * 256, 256)
            total = dot_tn(sel[h, :, pl.ds(at, 256)], back)
            for k in range(2):
                both = jnp.concatenate([hb[g, k], hb[g + 1, k]], axis=1)
                total = total + dot_tn(both, wt[k])
            dx[pl.ds(g, 2)] = total.astype(BF16).reshape(2, 4, 2, 16, COVER)

    def e_copy(xx, t, lanes):
        src = dx.at[pl.ds(4 * xx, 4), t // 2, t % 2, :, lanes]
        return rc(src, er.at[xx, tp, :, :, lanes], e_s.at[xx, t], e_r.at[xx, tp], (ep, t))

    def e_start(xx):
        @pl.loop(1, NT)
        def _(k):
            by_core(lambda lanes: e_copy(xx, (tp + k) % NT, lanes).start())

    def f_copy(j, lanes):
        return rc(fs.at[j, :, lanes], fb.at[ep, :, lanes], f_s.at[j], f_r.at[ep], (j, tp))

    def e_last(xx):
        @pl.loop(1, NT)
        def _(k):
            t = (tp + k) % NT
            by_core(lambda lanes: got(er.at[xx, t, :, :, lanes], e_r.at[xx, t]))

        er[xx, tp] = dx[pl.ds(4 * xx, 4), y, zl]
        total = er[xx, 0].astype(F32)
        for t in range(1, NT):
            total = total + er[xx, t].astype(F32)
        fs[pl.ds(4 * xx, 4)] = total.astype(BF16)

        @pl.loop(0, 4)
        def _(n):
            j = 4 * xx + (ep + n) % 4

            @pl.when(j != ep)
            def _():
                by_core(lambda lanes: f_copy(j, lanes).start())

            @pl.when(j == ep)
            def _():
                fb[j] = fs[j]

    def g_copy():
        return rc(gdense.at[:, :, 384:512], gx, k_s.at[1], k_r.at[1], dev_core)

    def weight_grads(k):
        gacc[...] = jnp.zeros((FFB, COVER), F32)

        @pl.loop(0, 4)
        def _(n):
            left = jnp.concatenate([hb[4 * n + m, k] for m in range(4)], axis=1)
            rows = xy[0 if k < 2 else 1, pl.ds(4 * n, 4)].reshape(4 * GROUP, COVER)
            gacc[...] += dot_nn(left, rows)

        gdense[k] = (gacc[...] * scale_dense).astype(BF16)
        if k == 2:
            pl.when(c == 0)(lambda: g_copy().start())

    got_a(0)
    b_zero(0)
    b_first(0, 0)
    b_first(0, 1)
    got_a(1)
    b_zero(1)
    slots()
    b_mid(0, 0)
    b_forward(0, 0, False)
    b_forward(0, 0, True)
    b_mid(0, 1)
    b_first(1, 0)
    b_forward(0, 1, False)
    b_end(0, 0)
    routed(0, 0)
    b_forward(0, 1, True)
    b_mid(1, 0)
    b_first(1, 1)
    b_end(0, 1)
    w_join()
    products(0)
    b_forward(1, 0, False)
    sum_core(0)
    c1_first(0)
    b_forward(1, 0, True)
    routed(0, 1)
    b_mid(1, 1)
    b_forward(1, 1, False)
    c1_second(0)
    b_end(1, 0)
    routed(1, 0)
    b_forward(1, 1, True)
    b_end(1, 1)
    routed(1, 1)
    products(1)
    c1_third(0)
    sum_core(1)
    c1_first(1)
    expert_forward(0)
    c1_second(1)
    expert_back(0)
    c1_third(1)
    d_first()
    expert_forward(1)
    expert_back(1)
    d_mid()
    d_forward()

    outs = []
    for a in range(2):
        for p in range(8):
            for m, lanes in enumerate((full, rest)):
                at = 896 * p + 512 * m
                outs.append(
                    pltpu.make_async_copy(
                        mr.at[a, 2 * p + m, :, lanes], erows.at[a, :, at : at + 512 - 128 * m], osem.at[a, 2 * p + m]
                    )
                )
    for o in outs:
        o.start()

    d_sides()
    d_core(0, x)
    got_back(0)
    got_back(1)
    input_grads(x)
    e_start(x)
    d_core(2, xs)
    d_core(4, xr)
    input_grads(xr)
    e_start(xr)
    d_far()
    input_grads(xs)
    e_start(xs)
    d_core(6, xo)
    input_grads(xo)
    e_start(xo)
    weight_grads(0)
    e_last(x)
    weight_grads(1)
    e_last(xr)
    weight_grads(2)
    e_last(xs)
    e_last(xo)

    @pl.loop(1, NE)
    def _(k):
        i = (ep + k) % NE
        pl.when(i % 2 == 0)(lambda: got(fb.at[i], f_r.at[i]))
        pl.when(i % 2 == 1)(lambda: got(fb.at[i, :, rest], f_r.at[i]))

    for p in range(8):
        for m, lanes in enumerate((full, rest)):
            at = slice(896 * p + 512 * m, 896 * p + 512 + 384 * m)
            gtok[:, at] = (cot[:, at].astype(F32) + fb[2 * p + m, :, lanes].astype(F32)).astype(BF16)

    @pl.when(c == 1)
    def _():
        got(gx, k_r.at[1])
        gdense[:, :, 0:128] = gx[...]

    for o in outs:
        o.wait()

    @pl.loop(1, NE)
    def _(k):
        j = (ep + k) % NE
        for a in range(2):
            pl.when(j % 2 == 0)(lambda: a_copy(a, k)(full).wait_send())
            pl.when(j % 2 == 1)(lambda: a_copy(a, k)(rest).wait_send())
        sent(route, r_s.at[k])
        by_core(lambda lanes: f_copy(j, lanes).wait_send())
        for h in range(2):
            for a in range(2):

                @pl.when(c == 0)
                def _():
                    m_copy(a, h, j, full).wait_send()

                @pl.when(c == 1)
                def _():
                    m_copy(a, h, j, rest).wait_send()

            @pl.when(j % 2 == 0)
            def _():
                back_copy(h, j, full).wait_send()

            @pl.when(j % 2 == 1)
            def _():
                back_copy(h, j, rest).wait_send()

    for a in range(2):
        for h in range(2):
            for n in range(7):
                sent_b(a, h, n)

        k0, k1 = spans[a]

        @pl.loop(0, 8)
        def _(p):
            sent(c0r.at[p // 2, p % 2, k0:k1], c0_s.at[a, p])

        for s in c1_sends(a):
            s.wait_send()
        c2_send(a).wait_send()

    @pl.loop(0, 15)
    def _(n):
        sent(h_at(x, zh), d_s.at[n])

    @pl.loop(1, NT)
    def _(k):
        for n in range(4):
            by_core(lambda lanes: e_copy(n, (tp + k) % NT, lanes).wait_send())

    @pl.when(c == 0)
    def _():
        g_copy().wait_send()

    @pl.when(c == 1)
    def _():
        w_copy().wait_send()


def exchange(tokens, cotangent, ids, probs, dgate, dup, ddown, eg, eu, ed, scale_dense):
    vm = lambda shape, dt=BF16: pltpu.VMEM(shape, dt)
    dma = lambda *shape: pltpu.SemaphoreType.DMA(shape)
    width = tokens.shape[1]
    vspec = pl.BlockSpec(memory_space=pltpu.VMEM)
    hspec = pl.BlockSpec(memory_space=pl.ANY)
    return pl.pallas_call(
        functools.partial(kernel, scale_dense),
        name="exchange",
        out_shape=(
            jax.ShapeDtypeStruct(tokens.shape, BF16),
            jax.ShapeDtypeStruct((3, FFB, COVER), BF16),
            jax.ShapeDtypeStruct((3, SLOTS, HID), BF16),
            jax.ShapeDtypeStruct((2, SLOTS, width), BF16),
        ),
        in_specs=[vspec] * 7 + [hspec] * 3,
        out_specs=(vspec, vspec, vspec, hspec),
        scratch_shapes=[
            vm((2, NE, 4, 2, 16, COVER)),
            vm((8, GROUP), F32),
            vm((NE, 8, GROUP), F32),
            vm((3, FFB, COVER)),
            vm((3, FFB, 128)),
            vm((3, FFB, 128)),
            vm((NE, 3, FFB, GROUP)),
            vm((4, 2, 3, FFB, GROUP)),
            vm((2, 3, FFB, GROUP)),
            vm((2, 2, 3, FFB, GROUP)),
            vm((3, FFB, GROUP)),
            vm((NE, 3, FFB, GROUP)),
            vm((2, NE * HALF_SLOTS, 8 * GROUP)),
            vm((2, NE * HALF_SLOTS, 128), F32),
            vm((2, NE, SLOTS, COVER)),
            vm((2, NE, SLOTS, COVER)),
            vm((3, HID, width)),
            vm((3, HALF_SLOTS, HID), F32),
            vm((NE, SLOTS, COVER)),
            vm((NE, SLOTS, COVER)),
            vm((NE, 4, 2, 16, COVER)),
            vm((4, NT, 4, 16, COVER)),
            vm((NE, 16, COVER)),
            vm((NE, 16, COVER)),
            vm((FFB, COVER), F32),
            dma(3),
            dma(2, NE), dma(2, NE),
            dma(NE), dma(NE),
            dma(4, 7), dma(4, 7),
            dma(2, 8), dma(2, 8),
            dma(2, 3), dma(2, 3),
            dma(2), dma(2),
            dma(15), dma(15),
            dma(6, NE), dma(6, NE),
            dma(4, NT), dma(4, NT),
            dma(NE), dma(NE),
            dma(2), dma(2),
            dma(2, NE),
        ],
        compiler_params=pltpu.CompilerParams(
            collective_id=0, has_side_effects=True, vmem_limit_bytes=60 * 1024 * 1024
        ),
    )(tokens, cotangent, ids, probs, dgate, dup, ddown, eg, eu, ed)


def finish_kernel(scale_expert, gtok, gdense, eact, erows, otok, ogate, oup, odown, eg, eu, ed):
    odd = lax.axis_index("ep") % 2

    @pl.when((pl.program_id(0) == 0) & (odd == 0))
    def _():
        for k, o in enumerate((ogate, oup, odown)):
            o[...] = gdense[k, :, 0:448]

    @pl.when((pl.program_id(0) == 0) & (odd == 1))
    def _():
        for k, o in enumerate((ogate, oup, odown)):
            o[...] = gdense[k, :, 64:512]

    otok[...] = gtok[...]
    for k, o in enumerate((eg, eu, ed)):
        o[...] = (dot_tn(eact[k], erows[k // 2]) * scale_expert).astype(BF16)


def finish(gtok, gdense, eact, erows, scale_expert):
    rows, width = gtok.shape
    step = 3584
    whole = lambda *shape: pl.BlockSpec(shape, lambda n: (0,) * len(shape))
    by_step = lambda *shape: pl.BlockSpec(shape + (step,), lambda n: (0,) * len(shape) + (n,))
    return pl.pallas_call(
        functools.partial(finish_kernel, scale_expert),
        name="finish",
        grid=(width // step,),
        in_specs=[by_step(rows), whole(3, FFB, COVER), whole(3, SLOTS, HID), by_step(2, SLOTS)],
        out_specs=[by_step(rows)] + [whole(FFB, 448)] * 3 + [by_step(HID)] * 3,
        out_shape=[jax.ShapeDtypeStruct((rows, width), BF16)]
        + [jax.ShapeDtypeStruct((FFB, 448), BF16)] * 3
        + [jax.ShapeDtypeStruct((HID, width), BF16)] * 3,
        compiler_params=pltpu.CompilerParams(vmem_limit_bytes=60 * 1024 * 1024),
    )(gtok, gdense, eact, erows)


def per_device(
    tokens, cotangent, route_ids, route_probs, dense_gate, dense_up, dense_down, expert_gate, expert_up, expert_down
):
    total_tokens = NE * GROUP
    scale_dense = 1.0 / math.sqrt(total_tokens)
    scale_expert = math.sqrt(NE * NT // 2 / (2.0 * total_tokens))
    gtok, gdense, eact, erows = exchange(
        tokens, cotangent, route_ids.T, route_probs.T, dense_gate.T, dense_up.T, dense_down,
        expert_gate[0], expert_up[0], expert_down[0], scale_dense,
    )
    gtok, ggate, gup, gdown, eg, eu, ed = finish(gtok, gdense, eact, erows, scale_expert)
    return (gtok, ggate.T, gup.T, gdown, eg[None], eu[None], ed[None])


def solution(mesh):
    return jax.shard_map(
        per_device,
        mesh=mesh,
        in_specs=(
            P(("ep", "tp"), None),
            P(("ep", "tp"), None),
            P("ep", None),
            P("ep", None),
            P("ep", "tp"),
            P("ep", "tp"),
            P("tp", "ep"),
            P(("ep", "tp"), None, None),
            P(("ep", "tp"), None, None),
            P(("ep", "tp"), None, None),
        ),
        out_specs=(
            P(("ep", "tp"), None),
            P("ep", "tp"),
            P("ep", "tp"),
            P("tp", "ep"),
            P(("ep", "tp"), None, None),
            P(("ep", "tp"), None, None),
            P(("ep", "tp"), None, None),
        ),
        check_vma=False,
    )
```

```python
import functools
import math

import jax
import jax.numpy as jnp
from jax import lax
from jax.experimental import pallas as pl
from jax.experimental.pallas import tpu as pltpu
from jax.sharding import PartitionSpec as P

MESH = pl.DeviceIdType.MESH
F32 = jnp.float32
BF16 = jnp.bfloat16

NE, NT = 16, 8
GROUP, CAP = 128, 6
SLOTS = NE * CAP
HALF_SLOTS = SLOTS // 2
COVER = 512
FFB = 304
HID = 192


def dot_nt(a, b):
    return lax.dot_general(a, b, (((1,), (1,)), ((), ())), preferred_element_type=F32)


def dot_nn(a, b):
    return lax.dot_general(a, b, (((1,), (0,)), ((), ())), preferred_element_type=F32)


def dot_tn(a, b):
    return lax.dot_general(a, b, (((0,), (0,)), ((), ())), preferred_element_type=F32)


def unit_grads(gate_pre, up_pre, d_hidden):
    sigmoid_gate = jax.nn.sigmoid(gate_pre)
    activated = gate_pre * sigmoid_gate
    hidden = (activated * up_pre).astype(BF16)
    d_gate = (d_hidden * up_pre * sigmoid_gate * (1.0 + gate_pre * (1.0 - sigmoid_gate))).astype(BF16)
    d_up = (d_hidden * activated).astype(BF16)
    return hidden, d_gate, d_up


def kernel(
    scale_dense,
    tok, cot, ids, probs, dgate, dup, ddown, eg, eu, ed,
    gtok, gdense, eact, erows,
    xy, route, rr, wt, wx, gx, part, c0r, x1r, x2r, z2r, hb, sel, sprob, ms, mr, we, eacc, bs, rb, dx, er, fs, fb, gacc,
    wsem, a_s, a_r, r_s, r_r, b_s, b_r, c0_s, c0_rs, c1_s, c1_rs, c2_s, c2_rs, d_s, d_r, m_s, m_r, e_s, e_r, f_s, f_r, k_s, k_r, osem,
):
    ep, tp = lax.axis_index("ep"), lax.axis_index("tp")
    x, zh, c = ep // 4, (ep // 2) % 2, ep % 2
    y, zl = tp // 2, tp % 2
    xo, xs, xr = (x + 2) % 4, (x + 1 + 2 * c) % 4, (x + 3 + 2 * c) % 4
    yo, ys, yr = (y + 2) % 4, (y + 1 + 2 * c) % 4, (y + 3 + 2 * c) % 4

    full, rest = slice(0, COVER), slice(128, COVER)

    def by_core(act):
        pl.when(c == 0)(lambda: act(full))
        pl.when(c == 1)(lambda: act(rest))

    def dev_x(xx):
        return ((xx * 2 + zh) * 2 + c, tp)

    def dev_y(yy):
        return (ep, yy * 2 + zl)

    dev_zh = ((x * 2 + 1 - zh) * 2 + c, tp)
    dev_core = ((x * 2 + zh) * 2 + 1 - c, tp)
    dev_zl = (ep, y * 2 + 1 - zl)

    def rc(src, dst, s, r, dev):
        return pltpu.make_async_remote_copy(
            src_ref=src, dst_ref=dst, send_sem=s, recv_sem=r, device_id=dev, device_id_type=MESH
        )

    def got(ref, r):
        rc(ref, ref, r, r, dev_core).wait_recv()

    def sent(ref, s):
        rc(ref, ref, s, s, dev_core).wait_send()

    def add(dst, srcs_):
        total = dst[...].astype(F32)
        for s in srcs_:
            total = total + s[...].astype(F32)
        dst[...] = total.astype(BF16)

    loads = [pltpu.make_async_copy(w, we.at[n], wsem.at[n]) for n, w in enumerate((eg, eu, ed))]
    for w in loads:
        w.start()

    barrier = pltpu.get_barrier_semaphore()

    @pl.loop(1, NE)
    def _(k):
        pl.semaphore_signal(barrier, inc=1, device_id=((ep + k) % NE, tp), device_id_type=MESH)

    @pl.loop(1, NT)
    def _(k):
        pl.semaphore_signal(barrier, inc=1, device_id=(ep, (tp + k) % NT), device_id_type=MESH)


    @pl.when(c == 1)
    def _():
        rb[:, :, 0:128] = jnp.zeros((NE, SLOTS, 128), BF16)
        xy[:, :, :, :, :, 0:128] = jnp.zeros((2, NE, 4, 2, 16, 128), BF16)

    pl.semaphore_wait(barrier, NE - 1 + NT - 1)

    srcs = (tok, cot)

    def a_copy(a, k):
        j = (ep + k) % NE
        at = pl.multiple_of(896 * (j // 2) + 512 * (j % 2), 128)
        return lambda lanes: rc(
            srcs[a].at[:, pl.ds(at, lanes.stop - lanes.start)],
            xy.at[a, ep, y, zl, :, lanes], a_s.at[a, k], a_r.at[a, k], (j, tp),
        )

    def a_send(a):
        @pl.loop(1, NE)
        def _(k):
            pl.when((ep + k) % 2 == 0)(lambda: a_copy(a, k)(full).start())
            pl.when((ep + k) % 2 == 1)(lambda: a_copy(a, k)(rest).start())

        @pl.when(c == 0)
        def _():
            xy[a, ep, y, zl] = srcs[a][:, pl.ds(pl.multiple_of(896 * (ep // 2), 128), 512)]

        @pl.when(c == 1)
        def _():
            xy[a, ep, y, zl, :, 128:512] = srcs[a][:, pl.ds(pl.multiple_of(896 * (ep // 2) + 512, 128), 384)]

    a_send(0)

    before = lax.broadcasted_iota(jnp.int32, (GROUP, GROUP), 0) < lax.broadcasted_iota(jnp.int32, (GROUP, GROUP), 1)
    across = [jnp.broadcast_to(ids[k : k + 1, :].astype(F32), (GROUP, GROUP)) for k in range(2)]
    down = [jnp.transpose(m) for m in across]
    codes = []
    for k in range(2):
        rank = jnp.zeros((1, GROUP), F32)
        for m in down:
            rank = rank + jnp.sum(jnp.where(before & (m == across[k]), 1.0, 0.0), axis=0, keepdims=True)
        idk = ids[k : k + 1, :]
        group_at = (ep % 8) * CAP
        fixed = (idk & 3) * (NE * HALF_SLOTS) + (idk >> 2) * HALF_SLOTS + group_at
        codes.append(fixed.astype(F32) + rank)
    route[...] = jnp.concatenate([codes[0], codes[1], probs[...], jnp.zeros((4, GROUP), F32)], axis=0)

    @pl.loop(1, NE)
    def _(k):
        rc(route, rr.at[ep], r_s.at[k], r_r.at[k], ((ep + k) % NE, tp)).start()

    a_send(1)
    def w_copy():
        return rc(wt.at[:, :, 0:128], wx, k_s.at[0], k_r.at[0], dev_core)

    def w_join():
        @pl.when(c == 0)
        def _():
            got(wx, k_r.at[0])
            for k in range(3):
                wt[k, :, 384:512] = wt[k, :, 384:512] + wx[k]

    blank = jnp.zeros((FFB, COVER - 448), BF16)

    @pl.when(c == 0)
    def _():
        for k, w in enumerate((dgate, dup, ddown)):
            wt[k] = jnp.concatenate([w[...], blank], axis=1)

    @pl.when(c == 1)
    def _():
        for k, w in enumerate((dgate, dup, ddown)):
            wt[k] = jnp.concatenate([blank, w[...]], axis=1)
        w_copy().start()

    rr[ep] = route[...]

    def got_a(a):
        @pl.loop(1, NE)
        def _(k):
            i = (ep + NE - k) % NE
            by_core(lambda lanes: got(xy.at[a, i, y, zl, :, lanes], a_r.at[a, k]))

    def send_b(a, h, n, yy, zz, dev):
        def act(lanes):
            ref = xy.at[a, 8 * h : 8 * h + 8, yy, zz, :, lanes]
            rc(ref, ref, b_s.at[2 * a + h, n], b_r.at[2 * a + h, n], dev).start()

        by_core(act)

    def got_b(a, h, n, yy, zz):
        by_core(lambda lanes: got(xy.at[a, 8 * h : 8 * h + 8, yy, zz, :, lanes], b_r.at[2 * a + h, n]))

    def sent_b(a, h, n):
        by_core(lambda lanes: sent(xy.at[a, 8 * h : 8 * h + 8, y, zl, :, lanes], b_s.at[2 * a + h, n]))

    def b_zero(a):
        for h in range(2):
            send_b(a, h, 0, y, zl, dev_zl)

    def b_first(a, h):
        send_b(a, h, 1, y, zl, dev_y(ys))
        send_b(a, h, 2, y, zl, dev_y(yr))

    def b_mid(a, h):
        got_b(a, h, 0, y, 1 - zl)
        send_b(a, h, 3, y, 1 - zl, dev_y(ys))
        send_b(a, h, 4, y, 1 - zl, dev_y(yr))

    def b_forward(a, h, second):
        if second:
            got_b(a, h, 3, yr, 1 - zl)
            send_b(a, h, 6, yr, 1 - zl, dev_y(ys))
        else:
            got_b(a, h, 1, yr, zl)
            send_b(a, h, 5, yr, zl, dev_y(ys))
            got_b(a, h, 2, ys, zl)

    def b_end(a, h):
        got_b(a, h, 5, yo, zl)
        got_b(a, h, 4, ys, 1 - zl)
        got_b(a, h, 6, yo, 1 - zl)

    def slots():
        @pl.loop(1, NE)
        def _(k):
            got(rr.at[(ep + NE - k) % NE], r_r.at[k])

        base = ((tp // 2) * (NE * HALF_SLOTS)).astype(F32)
        for h in range(2):
            sprob[h] = jnp.zeros((NE * HALF_SLOTS, 128), F32)

            @pl.loop(0, 8)
            def _(gl):
                row = rr[h * 8 + gl]
                numbers = lax.broadcasted_iota(jnp.int32, (NE * HALF_SLOTS, 128), 0).astype(F32)
                first = numbers == (row[0:1] - base)
                second = numbers == (row[1:2] - base)
                sel[h, :, pl.ds(pl.multiple_of(gl * 128, 128), 128)] = jnp.where(first | second, 1.0, 0.0).astype(BF16)
                sprob[h] += jnp.where(first, row[2:3], 0.0) + jnp.where(second, row[3:4], 0.0)

            sprob[h] = jnp.broadcast_to(jnp.sum(sprob[h], axis=1, keepdims=True), (NE * HALF_SLOTS, 128))

    spans = ((0, 2), (2, 3))

    def products(a):
        k0, k1 = spans[a]

        @pl.loop(0, 8)
        def _(p):
            def act(lanes):
                rows = xy[a, pl.ds(2 * p, 2), :, :, :, lanes].reshape(2 * GROUP, lanes.stop - lanes.start)
                for k in range(k0, k1):
                    res = dot_nt(wt[k, :, lanes], rows).astype(BF16)
                    part[2 * p, k] = res[:, :GROUP]
                    part[2 * p + 1, k] = res[:, GROUP:]

            by_core(act)
            rc(
                part.at[2 * p + 1 - c, k0:k1], c0r.at[p // 2, p % 2, k0:k1], c0_s.at[a, p], c0_rs.at[a, p], dev_core
            ).start()

    def sum_core(a):
        k0, k1 = spans[a]

        @pl.loop(0, 8)
        def _(p):
            got(c0r.at[p // 2, p % 2, k0:k1], c0_rs.at[a, p])
            for k in range(k0, k1):
                add(c0r.at[p // 2, p % 2, k], [part.at[2 * p + c, k]])

    def c1_sends(a):
        k0, k1 = spans[a]
        q = lambda xx: c0r.at[xx, :, k0:k1]
        return [
            rc(q(xo), x1r.at[:, k0:k1], c1_s.at[a, 0], c1_rs.at[a, 0], dev_x(xs)),
            rc(q(xr), x2r.at[1, :, k0:k1], c1_s.at[a, 1], c1_rs.at[a, 1], dev_x(xr)),
            rc(q(xs), x2r.at[0, :, k0:k1], c1_s.at[a, 2], c1_rs.at[a, 2], dev_x(xs)),
        ]

    def c1_first(a):
        for s in c1_sends(a)[:2]:
            s.start()

    def c1_second(a):
        k0, k1 = spans[a]
        sends = c1_sends(a)
        sends[0].wait_recv()
        for zz in range(2):
            for k in range(k0, k1):
                add(c0r.at[xs, zz, k], [x1r.at[zz, k]])
        sends[2].start()

    def c2_send(a):
        k0, k1 = spans[a]
        return rc(c0r.at[x, 1 - zh, k0:k1], z2r.at[k0:k1], c2_s.at[a], c2_rs.at[a], dev_zh)

    def c1_third(a):
        k0, k1 = spans[a]
        sends = c1_sends(a)
        for n in (1, 2):
            sends[n].wait_recv()
        for n, zz in enumerate((1 - zh, zh)):
            for k in range(k0, k1):
                add(c0r.at[x, zz, k], [x2r.at[0, zz, k], x2r.at[1, zz, k]])
            if n == 0:
                c2_send(a).start()

    def rows_of(h):
        return slice(HALF_SLOTS * h, HALF_SLOTS * (h + 1))

    def m_copy(a, h, j, lanes):
        return rc(
            ms.at[a, j, rows_of(h), lanes], mr.at[a, ep, rows_of(h), lanes], m_s.at[2 * a + h, j], m_r.at[2 * a + h, ep], (j, tp)
        )

    def routed(a, h):
        @pl.loop(0, 4)
        def _(n):
            jj = (x + n) % 4
            rows = xy[a, 8 * h : 8 * h + 8].reshape(8 * GROUP, COVER)
            at = pl.multiple_of(jj * 4 * HALF_SLOTS, 64)
            res = dot_nn(sel[h, pl.ds(at, 4 * HALF_SLOTS)], rows)
            if a == 1:
                res = res * sprob[h, pl.ds(at, 4 * HALF_SLOTS), 0:1]
            ms[a, pl.ds(jj * 4, 4), rows_of(h)] = res.astype(BF16).reshape(4, HALF_SLOTS, COVER)

            @pl.loop(0, 4)
            def _(m):
                j = jj * 4 + m

                @pl.when((j != ep) & (c == 0))
                def _():
                    m_copy(a, h, j, full).start()

                @pl.when((j != ep) & (c == 1))
                def _():
                    m_copy(a, h, j, rest).start()

                @pl.when(j == ep)
                def _():
                    mr[a, j, rows_of(h)] = ms[a, j, rows_of(h)]

    def got_routed(a, h):
        @pl.loop(0, 8)
        def _(p):
            @pl.when(2 * p != ep)
            def _():
                got(mr.at[a, 2 * p, rows_of(h)], m_r.at[2 * a + h, 2 * p])

            @pl.when(2 * p + 1 != ep)
            def _():
                got(mr.at[a, 2 * p + 1, rows_of(h), rest], m_r.at[2 * a + h, 2 * p + 1])

    def expert_forward(h):
        for a in range(2):
            got_routed(a, h)
        if h == 0:
            for w in loads:
                w.wait()
        for n, a in enumerate((0, 0, 1)):
            total = jnp.zeros((HALF_SLOTS, HID), F32)
            for p in range(8):
                total += dot_nt(mr[a, 2 * p, rows_of(h)], we[n, :, 896 * p : 896 * p + 512])
                total += dot_nt(mr[a, 2 * p + 1, rows_of(h), rest], we[n, :, 896 * p + 512 : 896 * p + 896])
            eacc[n] = total
        hidden, d_gate, d_up = unit_grads(eacc[0], eacc[1], eacc[2])
        eact[0, rows_of(h)] = d_gate
        eact[1, rows_of(h)] = d_up
        eact[2, rows_of(h)] = hidden

    def back_copy(h, i, lanes):
        return rc(bs.at[i, rows_of(h), lanes], rb.at[ep, rows_of(h), lanes], m_s.at[4 + h, i], m_r.at[4 + h, ep], (i, tp))

    def expert_back(h):
        @pl.loop(0, 8)
        def _(n):
            p = (ep // 2 + n) % 8
            g, u = eact[0, rows_of(h)], eact[1, rows_of(h)]
            for m, lanes in enumerate((full, rest)):
                i = 2 * p + m
                wide = pl.ds(pl.multiple_of(896 * p + 512 * m, 128), 512 - 128 * m)
                bs[i, rows_of(h), lanes] = (dot_nn(g, we[0, :, wide]) + dot_nn(u, we[1, :, wide])).astype(BF16)

                @pl.when(i != ep)
                def _():
                    back_copy(h, i, lanes).start()

                @pl.when(i == ep)
                def _():
                    rb[i, rows_of(h), lanes] = bs[i, rows_of(h), lanes]

    def got_back(h):
        @pl.loop(1, NE)
        def _(k):
            j = (ep + k) % NE

            @pl.when(c == 0)
            def _():
                got(rb.at[j, rows_of(h)], m_r.at[4 + h, j])

            @pl.when(c == 1)
            def _():
                got(rb.at[j, rows_of(h), rest], m_r.at[4 + h, j])

    def h_at(xx, zz):
        return hb.at[(xx * 2 + zz) * 2 + c]

    def send_d(n, xx, zz, dev):
        rc(h_at(xx, zz), h_at(xx, zz), d_s.at[n], d_r.at[n], dev).start()

    def got_d(n, xx, zz):
        got(h_at(xx, zz), d_r.at[n])

    def to_core(n, xx, zz):
        send_d(7 + n, xx, zz, dev_core)

    def d_first():
        for a in range(2):
            k0, k1 = spans[a]
            got(z2r.at[k0:k1], c2_rs.at[a])
        mine = [c0r[x, zh, k].astype(F32) + z2r[k].astype(F32) for k in range(3)]
        hidden, d_gate, d_up = unit_grads(*mine)
        hb[ep, 0] = d_gate
        hb[ep, 1] = d_up
        hb[ep, 2] = hidden
        send_d(0, x, zh, dev_zh)
        send_d(1, x, zh, dev_x(xs))
        send_d(2, x, zh, dev_x(xr))
        to_core(0, x, zh)

    def d_mid():
        got_d(0, x, 1 - zh)
        send_d(3, x, 1 - zh, dev_x(xs))
        send_d(4, x, 1 - zh, dev_x(xr))
        to_core(1, x, 1 - zh)

    def d_forward():
        got_d(1, xr, zh)
        send_d(5, xr, zh, dev_x(xs))
        to_core(2, xr, zh)
        got_d(3, xr, 1 - zh)
        send_d(6, xr, 1 - zh, dev_x(xs))
        to_core(3, xr, 1 - zh)

    def d_sides():
        got_d(2, xs, zh)
        to_core(4, xs, zh)
        got_d(4, xs, 1 - zh)
        to_core(5, xs, 1 - zh)

    def d_far():
        got_d(5, xo, zh)
        to_core(6, xo, zh)
        got_d(6, xo, 1 - zh)
        to_core(7, xo, 1 - zh)

    def d_core(n, xx):
        got(hb.at[(xx * 2 + zh) * 2 + 1 - c], d_r.at[7 + n])
        got(hb.at[(xx * 2 + 1 - zh) * 2 + 1 - c], d_r.at[8 + n])

    def input_grads(xx):
        h = xx // 2

        @pl.loop(0, 2)
        def _(n):
            g = 4 * xx + 2 * n
            back = rb[:, pl.ds(pl.multiple_of(HALF_SLOTS * h, 16), HALF_SLOTS)].reshape(NE * HALF_SLOTS, COVER)
            at = pl.multiple_of((xx % 2) * 512 + n * 256, 256)
            total = dot_tn(sel[h, :, pl.ds(at, 256)], back)
            for k in range(2):
                both = jnp.concatenate([hb[g, k], hb[g + 1, k]], axis=1)
                total = total + dot_tn(both, wt[k])
            dx[pl.ds(g, 2)] = total.astype(BF16).reshape(2, 4, 2, 16, COVER)

    def e_copy(xx, t, lanes):
        src = dx.at[pl.ds(4 * xx, 4), t // 2, t % 2, :, lanes]
        return rc(src, er.at[xx, tp, :, :, lanes], e_s.at[xx, t], e_r.at[xx, tp], (ep, t))

    def e_start(xx):
        @pl.loop(1, NT)
        def _(k):
            by_core(lambda lanes: e_copy(xx, (tp + k) % NT, lanes).start())

    def f_copy(j, lanes):
        return rc(fs.at[j, :, lanes], fb.at[ep, :, lanes], f_s.at[j], f_r.at[ep], (j, tp))

    def e_last(xx):
        @pl.loop(1, NT)
        def _(k):
            t = (tp + k) % NT
            by_core(lambda lanes: got(er.at[xx, t, :, :, lanes], e_r.at[xx, t]))

        er[xx, tp] = dx[pl.ds(4 * xx, 4), y, zl]
        total = er[xx, 0].astype(F32)
        for t in range(1, NT):
            total = total + er[xx, t].astype(F32)
        fs[pl.ds(4 * xx, 4)] = total.astype(BF16)

        @pl.loop(0, 4)
        def _(n):
            j = 4 * xx + (ep + n) % 4

            @pl.when(j != ep)
            def _():
                by_core(lambda lanes: f_copy(j, lanes).start())

            @pl.when(j == ep)
            def _():
                fb[j] = fs[j]

    def g_copy():
        return rc(gdense.at[:, :, 384:512], gx, k_s.at[1], k_r.at[1], dev_core)

    def weight_grads(k):
        gacc[...] = jnp.zeros((FFB, COVER), F32)

        @pl.loop(0, 4)
        def _(n):
            left = jnp.concatenate([hb[4 * n + m, k] for m in range(4)], axis=1)
            rows = xy[0 if k < 2 else 1, pl.ds(4 * n, 4)].reshape(4 * GROUP, COVER)
            gacc[...] += dot_nn(left, rows)

        gdense[k] = (gacc[...] * scale_dense).astype(BF16)
        if k == 2:
            pl.when(c == 0)(lambda: g_copy().start())

    got_a(0)
    b_zero(0)
    b_first(0, 0)
    b_first(0, 1)
    got_a(1)
    b_zero(1)
    slots()
    b_mid(0, 0)
    b_forward(0, 0, False)
    b_forward(0, 0, True)
    b_mid(0, 1)
    b_first(1, 0)
    b_forward(0, 1, False)
    b_end(0, 0)
    routed(0, 0)
    b_forward(0, 1, True)
    b_mid(1, 0)
    b_first(1, 1)
    b_end(0, 1)
    w_join()
    products(0)
    b_forward(1, 0, False)
    sum_core(0)
    c1_first(0)
    b_forward(1, 0, True)
    routed(0, 1)
    b_mid(1, 1)
    b_forward(1, 1, False)
    c1_second(0)
    b_end(1, 0)
    routed(1, 0)
    b_forward(1, 1, True)
    b_end(1, 1)
    routed(1, 1)
    products(1)
    c1_third(0)
    sum_core(1)
    c1_first(1)
    expert_forward(0)
    c1_second(1)
    expert_back(0)
    c1_third(1)
    d_first()
    expert_forward(1)
    expert_back(1)
    d_mid()
    d_forward()

    outs = []
    for a in range(2):
        for p in range(8):
            for m, lanes in enumerate((full, rest)):
                at = 896 * p + 512 * m
                outs.append(
                    pltpu.make_async_copy(
                        mr.at[a, 2 * p + m, :, lanes], erows.at[a, :, at : at + 512 - 128 * m], osem.at[a, 2 * p + m]
                    )
                )
    for o in outs:
        o.start()

    d_sides()
    d_core(0, x)
    got_back(0)
    got_back(1)
    input_grads(x)
    e_start(x)
    d_core(2, xs)
    d_core(4, xr)
    d_far()
    input_grads(xr)
    e_start(xr)
    input_grads(xs)
    e_start(xs)
    d_core(6, xo)
    input_grads(xo)
    e_start(xo)
    weight_grads(0)
    e_last(x)
    weight_grads(1)
    e_last(xr)
    weight_grads(2)
    e_last(xs)
    e_last(xo)

    @pl.loop(1, NE)
    def _(k):
        i = (ep + k) % NE
        pl.when(i % 2 == 0)(lambda: got(fb.at[i], f_r.at[i]))
        pl.when(i % 2 == 1)(lambda: got(fb.at[i, :, rest], f_r.at[i]))

    for p in range(8):
        for m, lanes in enumerate((full, rest)):
            at = slice(896 * p + 512 * m, 896 * p + 512 + 384 * m)
            gtok[:, at] = (cot[:, at].astype(F32) + fb[2 * p + m, :, lanes].astype(F32)).astype(BF16)

    @pl.when(c == 1)
    def _():
        got(gx, k_r.at[1])
        gdense[:, :, 0:128] = gx[...]

    for o in outs:
        o.wait()

    @pl.loop(1, NE)
    def _(k):
        j = (ep + k) % NE
        for a in range(2):
            pl.when(j % 2 == 0)(lambda: a_copy(a, k)(full).wait_send())
            pl.when(j % 2 == 1)(lambda: a_copy(a, k)(rest).wait_send())
        sent(route, r_s.at[k])
        by_core(lambda lanes: f_copy(j, lanes).wait_send())
        for h in range(2):
            for a in range(2):

                @pl.when(c == 0)
                def _():
                    m_copy(a, h, j, full).wait_send()

                @pl.when(c == 1)
                def _():
                    m_copy(a, h, j, rest).wait_send()

            @pl.when(j % 2 == 0)
            def _():
                back_copy(h, j, full).wait_send()

            @pl.when(j % 2 == 1)
            def _():
                back_copy(h, j, rest).wait_send()

    for a in range(2):
        for h in range(2):
            for n in range(7):
                sent_b(a, h, n)

        k0, k1 = spans[a]

        @pl.loop(0, 8)
        def _(p):
            sent(c0r.at[p // 2, p % 2, k0:k1], c0_s.at[a, p])

        for s in c1_sends(a):
            s.wait_send()
        c2_send(a).wait_send()

    @pl.loop(0, 15)
    def _(n):
        sent(h_at(x, zh), d_s.at[n])

    @pl.loop(1, NT)
    def _(k):
        for n in range(4):
            by_core(lambda lanes: e_copy(n, (tp + k) % NT, lanes).wait_send())

    @pl.when(c == 0)
    def _():
        g_copy().wait_send()

    @pl.when(c == 1)
    def _():
        w_copy().wait_send()


def exchange(tokens, cotangent, ids, probs, dgate, dup, ddown, eg, eu, ed, scale_dense):
    vm = lambda shape, dt=BF16: pltpu.VMEM(shape, dt)
    dma = lambda *shape: pltpu.SemaphoreType.DMA(shape)
    width = tokens.shape[1]
    vspec = pl.BlockSpec(memory_space=pltpu.VMEM)
    hspec = pl.BlockSpec(memory_space=pl.ANY)
    return pl.pallas_call(
        functools.partial(kernel, scale_dense),
        name="exchange",
        out_shape=(
            jax.ShapeDtypeStruct(tokens.shape, BF16),
            jax.ShapeDtypeStruct((3, FFB, COVER), BF16),
            jax.ShapeDtypeStruct((3, SLOTS, HID), BF16),
            jax.ShapeDtypeStruct((2, SLOTS, width), BF16),
        ),
        in_specs=[vspec] * 7 + [hspec] * 3,
        out_specs=(vspec, vspec, vspec, hspec),
        scratch_shapes=[
            vm((2, NE, 4, 2, 16, COVER)),
            vm((8, GROUP), F32),
            vm((NE, 8, GROUP), F32),
            vm((3, FFB, COVER)),
            vm((3, FFB, 128)),
            vm((3, FFB, 128)),
            vm((NE, 3, FFB, GROUP)),
            vm((4, 2, 3, FFB, GROUP)),
            vm((2, 3, FFB, GROUP)),
            vm((2, 2, 3, FFB, GROUP)),
            vm((3, FFB, GROUP)),
            vm((NE, 3, FFB, GROUP)),
            vm((2, NE * HALF_SLOTS, 8 * GROUP)),
            vm((2, NE * HALF_SLOTS, 128), F32),
            vm((2, NE, SLOTS, COVER)),
            vm((2, NE, SLOTS, COVER)),
            vm((3, HID, width)),
            vm((3, HALF_SLOTS, HID), F32),
            vm((NE, SLOTS, COVER)),
            vm((NE, SLOTS, COVER)),
            vm((NE, 4, 2, 16, COVER)),
            vm((4, NT, 4, 16, COVER)),
            vm((NE, 16, COVER)),
            vm((NE, 16, COVER)),
            vm((FFB, COVER), F32),
            dma(3),
            dma(2, NE), dma(2, NE),
            dma(NE), dma(NE),
            dma(4, 7), dma(4, 7),
            dma(2, 8), dma(2, 8),
            dma(2, 3), dma(2, 3),
            dma(2), dma(2),
            dma(15), dma(15),
            dma(6, NE), dma(6, NE),
            dma(4, NT), dma(4, NT),
            dma(NE), dma(NE),
            dma(2), dma(2),
            dma(2, NE),
        ],
        compiler_params=pltpu.CompilerParams(
            collective_id=0, has_side_effects=True, vmem_limit_bytes=60 * 1024 * 1024
        ),
    )(tokens, cotangent, ids, probs, dgate, dup, ddown, eg, eu, ed)


def finish_kernel(scale_expert, gtok, gdense, eact, erows, otok, ogate, oup, odown, eg, eu, ed):
    odd = lax.axis_index("ep") % 2

    @pl.when((pl.program_id(0) == 0) & (odd == 0))
    def _():
        for k, o in enumerate((ogate, oup, odown)):
            o[...] = gdense[k, :, 0:448]

    @pl.when((pl.program_id(0) == 0) & (odd == 1))
    def _():
        for k, o in enumerate((ogate, oup, odown)):
            o[...] = gdense[k, :, 64:512]

    otok[...] = gtok[...]
    for k, o in enumerate((eg, eu, ed)):
        o[...] = (dot_tn(eact[k], erows[k // 2]) * scale_expert).astype(BF16)


def finish(gtok, gdense, eact, erows, scale_expert):
    rows, width = gtok.shape
    step = 3584
    whole = lambda *shape: pl.BlockSpec(shape, lambda n: (0,) * len(shape))
    by_step = lambda *shape: pl.BlockSpec(shape + (step,), lambda n: (0,) * len(shape) + (n,))
    return pl.pallas_call(
        functools.partial(finish_kernel, scale_expert),
        name="finish",
        grid=(width // step,),
        in_specs=[by_step(rows), whole(3, FFB, COVER), whole(3, SLOTS, HID), by_step(2, SLOTS)],
        out_specs=[by_step(rows)] + [whole(FFB, 448)] * 3 + [by_step(HID)] * 3,
        out_shape=[jax.ShapeDtypeStruct((rows, width), BF16)]
        + [jax.ShapeDtypeStruct((FFB, 448), BF16)] * 3
        + [jax.ShapeDtypeStruct((HID, width), BF16)] * 3,
        compiler_params=pltpu.CompilerParams(vmem_limit_bytes=60 * 1024 * 1024),
    )(gtok, gdense, eact, erows)


def per_device(
    tokens, cotangent, route_ids, route_probs, dense_gate, dense_up, dense_down, expert_gate, expert_up, expert_down
):
    total_tokens = NE * GROUP
    scale_dense = 1.0 / math.sqrt(total_tokens)
    scale_expert = math.sqrt(NE * NT // 2 / (2.0 * total_tokens))
    gtok, gdense, eact, erows = exchange(
        tokens, cotangent, route_ids.T, route_probs.T, dense_gate.T, dense_up.T, dense_down,
        expert_gate[0], expert_up[0], expert_down[0], scale_dense,
    )
    gtok, ggate, gup, gdown, eg, eu, ed = finish(gtok, gdense, eact, erows, scale_expert)
    return (gtok, ggate.T, gup.T, gdown, eg[None], eu[None], ed[None])


def solution(mesh):
    return jax.shard_map(
        per_device,
        mesh=mesh,
        in_specs=(
            P(("ep", "tp"), None),
            P(("ep", "tp"), None),
            P("ep", None),
            P("ep", None),
            P("ep", "tp"),
            P("ep", "tp"),
            P("tp", "ep"),
            P(("ep", "tp"), None, None),
            P(("ep", "tp"), None, None),
            P(("ep", "tp"), None, None),
        ),
        out_specs=(
            P(("ep", "tp"), None),
            P("ep", "tp"),
            P("ep", "tp"),
            P("tp", "ep"),
            P(("ep", "tp"), None, None),
            P(("ep", "tp"), None, None),
            P(("ep", "tp"), None, None),
        ),
        check_vma=False,
    )
```
